256 devices in a mesh: section: 2 (over core), tensor: 32 (over x, z), dp: 4 (over y).
Axes of the slice: x: 4, y: 4, z: 8, core: 2. Of those that a mesh axis runs over, the one named last changes fastest.
Arguments:
- grad_out: bfloat16 [2, 4, 512, 6144], P('section', 'dp', 'tensor'), may hold values from -6 to 6
- drop_seed: int32 [2], P('section'), may hold values from 0 to 1048575
- layer_in: bfloat16 [2, 4, 512, 6144], P('section', 'dp', 'tensor')
- ln_gain: float32 [2, 6144], P('section'), may hold values from 0.1 to 1.9
- pre_act: bfloat16 [2, 4, 512, 24576], P('section', 'dp', None, 'tensor'), may hold values from -6 to 6
- fc1_weight: bfloat16 [2, 24576, 6144], P('section', 'tensor', 'dp'), may hold values from -0.078125 to 0.078125
- fc2_weight: bfloat16 [2, 6144, 24576], P('section', 'dp', 'tensor'), may hold values from -0.0390625 to 0.0390625
Outputs:
- arriving_grad: bfloat16 [2, 4, 512, 6144], P('section', 'dp', 'tensor')
- fc2_weight_grad: bfloat16 [2, 6144, 24576], P('section', 'dp', 'tensor')
The draws below stay inside these ranges and needn't reach their ends.
All inputs are finite; a program needn't handle non-finite values.
Results may differ from the reference program's by a relative error of at most 0.013.
Values may be sent and summed in bfloat16 or wider, within the bound.
A program may use at most 128 MiB of HBM per device.

```python
import jax
import jax.numpy as jnp
from jax import lax

D = 6144
FF = 24576
SECTIONS = 2
REPLICAS = 4
TOK = 512


def draw_layer_in(key, part):
    key = jax.random.fold_in(key, 11)
    key_rows, key_cols, key_base = jax.random.split(key, 3)
    shape = (SECTIONS, REPLICAS, TOK, D)
    row_scale = jnp.exp(jax.random.uniform(key_rows, (SECTIONS, REPLICAS, TOK, 1), jnp.float32, 0.0, 2.4))
    col_scale = jnp.exp(jax.random.uniform(key_cols, (SECTIONS, 1, 1, D), jnp.float32, -1.2, 1.2))
    base = jax.random.normal(key_base, shape, jnp.float32)
    return (base * row_scale * col_scale).astype(jnp.bfloat16)


def block_scale(own_key, shape, pieces, low, top_value):
    level = 1.0
    for dim, parts in pieces:
        steps = jax.random.uniform(jax.random.fold_in(jax.random.fold_in(own_key, 6), dim), (parts,), jnp.float32, low / len(pieces), top_value / len(pieces))
        level = level * jnp.repeat(jnp.exp(steps), shape[dim] // parts).reshape((-1,) + (1,) * (len(shape) - 1 - dim))
    return level


def noise(rng, extent, spread, bound, cuts=(), dtype=jnp.bfloat16):
    values = spread * jax.random.normal(rng, extent, jnp.float32)
    if cuts:
        values = values * block_scale(rng, extent, cuts, -0.22, 0.18)
    return jnp.clip(values, -bound, bound).astype(dtype)


def setup_inputs(seed: int = 0) -> dict:
    arg_keys = jax.random.split(jax.random.key(seed), 8)
    return {
        "grad_out": noise(arg_keys[0], (SECTIONS, REPLICAS, TOK, D), 1.0, 6.0, ((0, 2), (1, 4), (2, 32))),
        "drop_seed": jax.random.randint(arg_keys[1], (SECTIONS,), 0, 1048576).astype(jnp.int32),
        "layer_in": draw_layer_in(jax.random.fold_in(arg_keys[7], 71), 0),
        "ln_gain": jnp.clip(1.0 + 0.18 * jax.random.normal(arg_keys[3], (SECTIONS, D), jnp.float32), 0.1, 1.9),
        "pre_act": noise(arg_keys[4], (SECTIONS, REPLICAS, TOK, FF), 1.0, 6.0, ((0, 2), (1, 4), (3, 32))),
        "fc1_weight": noise(arg_keys[5], (SECTIONS, FF, D), D ** -0.5, 0.078125, ((0, 2), (1, 32), (2, 4))),
        "fc2_weight": noise(arg_keys[6], (SECTIONS, D, FF), FF ** -0.5, 0.0390625, ((0, 2), (1, 4), (2, 32))),
    }


KEEP_SCALE = 1.0 / 0.9
NORM_EPS = 1e-05

def scramble(hashed):
    hashed = hashed * jnp.int32(739982445)
    hashed = hashed ^ jnp.right_shift(hashed, 15) & jnp.int32(131071)
    hashed = hashed * jnp.int32(695872825)
    hashed = hashed ^ jnp.right_shift(hashed, 13) & jnp.int32(524287)
    return hashed

def keep_table(seed_value, replica, first_row, row_count, feature_count):
    row_ids = (first_row + lax.iota(jnp.int32, row_count)).astype(jnp.int32)
    columns = lax.iota(jnp.int32, feature_count)
    offset = ((seed_value * jnp.int32(131) + replica) * jnp.int32(1640531527)).astype(jnp.int32)
    hashed = scramble((row_ids[:, None] * jnp.int32(feature_count) + columns[None, :] + offset).astype(jnp.int32))
    return jnp.right_shift(hashed, 9) & jnp.int32(1023) < jnp.int32(922)

def norm_back(upstream, normed_grad, layer_rows, gain):
    values = layer_rows.astype(jnp.float32)
    center = values - lax.optimization_barrier(jnp.mean(values, axis=-1, keepdims=True))
    inv_std = lax.rsqrt(lax.optimization_barrier(jnp.mean(center * center, axis=-1, keepdims=True)) + NORM_EPS)
    x_hat = center * inv_std
    scaled = normed_grad * gain
    bracket = scaled - lax.optimization_barrier(jnp.mean(scaled, axis=-1, keepdims=True)) - x_hat * lax.optimization_barrier(jnp.mean(scaled * x_hat, axis=-1, keepdims=True))
    return (upstream.astype(jnp.float32) + inv_std * bracket).astype(jnp.bfloat16)

def reference(grad_out, drop_seed, layer_in, ln_gain, pre_act, fc1_weight, fc2_weight):
    arriving = []
    weight_grads = []
    for section_id in range(SECTIONS):
        running = jnp.zeros((D, FF), jnp.float32)
        section_grads = []
        for replica in range(REPLICAS):
            upstream = grad_out[section_id, replica]
            kept_cells = keep_table(drop_seed[section_id], jnp.int32(replica), jnp.int32(0), TOK, D)
            factor = jnp.where(kept_cells, jnp.float32(KEEP_SCALE), jnp.float32(0.0))
            branch_grad = (upstream.astype(jnp.float32) * factor).astype(jnp.bfloat16)
            hidden_grad = jnp.dot(branch_grad, fc2_weight[section_id], preferred_element_type=jnp.float32)
            pre_rows = pre_act[section_id, replica]
            act_grad = jnp.where(pre_rows > 0, hidden_grad, jnp.float32(0.0)).astype(jnp.bfloat16)
            normed_grad = jnp.dot(act_grad, fc1_weight[section_id], preferred_element_type=jnp.float32)
            section_grads.append(norm_back(upstream, normed_grad, layer_in[section_id, replica], ln_gain[section_id]))
            hidden = jnp.maximum(pre_rows, 0)
            partial_value = jnp.dot(branch_grad.T, hidden, preferred_element_type=jnp.float32).astype(jnp.bfloat16)
            running = running + lax.optimization_barrier(partial_value).astype(jnp.float32)
        weight_grads.append(running.astype(jnp.bfloat16))
        arriving.append(jnp.stack(section_grads))
    arriving = jnp.stack(arriving)
    return (jnp.roll(arriving, -1, axis=0), jnp.stack(weight_grads))
```

```python
import functools

import jax
import jax.numpy as jnp
from jax import lax
from jax.experimental import pallas as pl
from jax.experimental.pallas import tpu as pltpu
from jax.sharding import PartitionSpec as P

KEEP_SCALE = 1.0 / 0.9
NORM_EPS = 1e-05
MESH = pl.DeviceIdType.MESH
X, Z, Y = 4, 8, 4
BF, F32 = jnp.bfloat16, jnp.float32

AG_A, AG_B, YR, RS_A, RS_B, WG, HF, LN0 = range(8)


def default_order():
    order = [(HF, 0, 0)]
    for tick in range(7 + Y - 1):
        for m in range(Y):
            k = tick - m
            if 0 <= k < 7:
                order += [(AG_A, m, k), (AG_B, m, k)]
                if k == 6:
                    order += [(YR, m, 0)]
        if tick == 3:
            order += [(HF, 0, 1)]
    order += [(HF, 0, 2), (LN0, 0, 0)]
    fill = list(range(6))
    for tick in range(4 + Y - 1 + 7):
        for m in range(Y):
            k = tick - m
            if 0 <= k < 4:
                order += [(YR, m, k + 1)]
            if 4 <= k < 11:
                order += [(RS_A, m, k - 4), (RS_B, m, k - 4)]
        if fill:
            order += [(WG, fill.pop(0), 0)]
    return order


ORDER = default_order()


def scramble(hashed):
    hashed = hashed * jnp.int32(739982445)
    hashed = hashed ^ jnp.right_shift(hashed, 15) & jnp.int32(131071)
    hashed = hashed * jnp.int32(695872825)
    hashed = hashed ^ jnp.right_shift(hashed, 13) & jnp.int32(524287)
    return hashed


def kernel(
    cols_a, seed_ref, grad_ref, layer_ref, gain_ref, pre_hbm, w1_hbm, w2_hbm,
    out_hbm, wg_hbm,
    branch, G, H, W1, W2, PH, RY1, RY2, ACT, N, RA4, RA, RAX2, RAX1, RB2, RB1, RBZ4, RBZ,
    WGR, xhat, inv, final, result, ssem, rsem, lsem,
):
    s = lax.axis_index("section")
    t = lax.axis_index("tensor")
    q = lax.axis_index("dp")
    x, z = t // Z, t % Z
    rows = grad_ref.shape[0]
    width = grad_ref.shape[1]
    block = width // Y
    hidden_cols = H.shape[-1]
    tok = H.shape[1]
    shard = tok // Y
    half = shard // 2
    A, B = pl.ds(0, cols_a), pl.ds(cols_a, block - cols_a)

    def xi(d):
        return (x + d + X) % X

    def zi(d):
        return (z + d + Z) % Z

    def yi(d):
        return (q + d + Y) % Y

    to = {
        "x+": (s, xi(1) * Z + z, q),
        "x-": (s, xi(-1) * Z + z, q),
        "z+": (s, x * Z + zi(1), q),
        "z-": (s, x * Z + zi(-1), q),
        "y+": (s, t, yi(1)),
        "y-": (s, t, yi(-1)),
        "y2": (s, t, yi(2)),
        "c": (1 - s, t, q),
    }
    copies = []
    pending = []

    def send(src, dst, where):
        i = len(copies)
        c = pltpu.make_async_remote_copy(
            src_ref=src, dst_ref=dst, send_sem=ssem.at[i], recv_sem=rsem.at[i],
            device_id=to[where], device_id_type=MESH,
        )
        copies.append(c)
        pending.append(c)
        c.start()
        return c

    def drain():
        for c in pending:
            c.wait_send()
        pending.clear()

    load_pre = pltpu.make_async_copy(pre_hbm, H.at[q], lsem.at[0])
    load_w2 = pltpu.make_async_copy(w2_hbm, W2, lsem.at[1])
    load_w1 = pltpu.make_async_copy(w1_hbm, W1, lsem.at[2])
    load_pre.start()
    load_w2.start()
    load_w1.start()

    barrier = pltpu.get_barrier_semaphore()
    for where in to.values():
        pl.semaphore_signal(barrier, inc=1, device_id=where, device_id_type=MESH)

    offset = (seed_ref[0] * jnp.int32(131) + q) * jnp.int32(1640531527)
    row_ids = t * rows + lax.broadcasted_iota(jnp.int32, (rows, block), 0)
    col_ids = lax.broadcasted_iota(jnp.int32, (rows, block), 1)
    base = row_ids * jnp.int32(width) + col_ids + offset
    for j in range(Y):
        hashed = scramble(base + jnp.int32(j * block))
        kept = (jnp.right_shift(hashed, 9) & jnp.int32(1023)) < jnp.int32(922)
        factor = jnp.where(kept, F32(KEEP_SCALE), F32(0.0))
        branch[j] = (grad_ref[:, j * block:(j + 1) * block].astype(F32) * factor).astype(BF)

    pl.semaphore_wait(barrier, len(to))

    first = []
    for d, where in ((1, "y+"), (3, "y-"), (2, "y2")):
        first.append(send(branch.at[yi(d)], G.at[q, x, z], where))
    G[q, x, z] = branch[q]
    load_pre.wait()
    H[q] = jnp.maximum(H[q], jnp.zeros((), BF))

    st = {}

    def hidden_step(k):
        if k == 0:
            st["h1"] = (send(H.at[q], H.at[q], "y+"), send(H.at[q], H.at[q], "y-"))
        elif k == 1:
            p, n = st["h1"]
            lo, hi = pl.ds(0, tok // 2), pl.ds(tok // 2, tok // 2)
            p.wait_recv()
            c0 = send(H.at[yi(-1), lo], H.at[yi(-1), lo], "y+")
            n.wait_recv()
            c1 = send(H.at[yi(1), hi], H.at[yi(1), hi], "y-")
            st["h2"] = (c0, c1)
        else:
            for c in st["h2"]:
                c.wait_recv()

    def wait2(key):
        for c in st.pop(key):
            c.wait_recv()

    def same(ref, where):
        return send(ref, ref, where)

    def ag_a(m, k):
        key = ("aga", m)
        if k > 0:
            wait2(key)
        if k == 0:
            own = G.at[m, x, z, :, A]
            st[key] = (same(own, "x+"), same(own, "x-"))
        elif k == 1:
            if m % 2 == 0:
                st[key] = (same(G.at[m, xi(-1), z, :, A], "x+"),)
            else:
                st[key] = (same(G.at[m, xi(1), z, :, A], "x-"),)
        elif k < 5:
            d = k - 2
            st[key] = (
                same(G.at[m, :, zi(-d), :, A], "z+"),
                same(G.at[m, :, zi(d), :, A], "z-"),
            )
        elif k == 5:
            st[key] = (
                same(G.at[m, pl.ds(0, 2), zi(-3), :, A], "z+"),
                same(G.at[m, pl.ds(2, 2), zi(3), :, A], "z-"),
            )

    def ag_b(m, k):
        key = ("agb", m)
        if k > 0:
            wait2(key)
        if k < 3:
            st[key] = (
                same(G.at[m, x, zi(-k), :, B], "z+"),
                same(G.at[m, x, zi(k), :, B], "z-"),
            )
        elif k == 3:
            if m % 2 == 0:
                st[key] = (same(G.at[m, x, zi(-3), :, B], "z+"),)
            else:
                st[key] = (same(G.at[m, x, zi(3), :, B], "z-"),)
        elif k == 4:
            own = G.at[m, x, :, :, B]
            st[key] = (same(own, "x+"), same(own, "x-"))
        elif k == 5:
            st[key] = (
                same(G.at[m, xi(-1), pl.ds(0, 4), :, B], "x+"),
                same(G.at[m, xi(1), pl.ds(4, 4), :, B], "x-"),
            )

    def y_step(m, k):
        key = ("y", m)
        if k > 0:
            wait2(key)
        lo, hi = pl.ds(0, half), pl.ds(half, half)
        if k == 0:
            if m == 0:
                load_w2.wait()
            tile = 256

            @pl.loop(0, hidden_cols // tile)
            def _(n):
                cols = pl.ds(pl.multiple_of(n * tile, tile), tile)
                part = jnp.dot(
                    G[m].reshape(tok, block), W2[:, cols], preferred_element_type=F32
                )
                PH[m, :, :, cols] = part.astype(BF).reshape(Y, shard, tile)

            st[key] = (
                send(PH.at[m, yi(2), lo], RY1.at[m, 0], "y+"),
                send(PH.at[m, yi(2), hi], RY1.at[m, 1], "y-"),
            )
        elif k == 1:
            PH[m, yi(1), lo] = (PH[m, yi(1), lo].astype(F32) + RY1[m, 0].astype(F32)).astype(BF)
            PH[m, yi(-1), hi] = (PH[m, yi(-1), hi].astype(F32) + RY1[m, 1].astype(F32)).astype(BF)
            st[key] = (
                send(PH.at[m, yi(1)], RY2.at[m, 0], "y+"),
                send(PH.at[m, yi(-1)], RY2.at[m, 1], "y-"),
            )
        elif k == 2:
            total = PH[m, q].astype(F32) + RY2[m, 0].astype(F32) + RY2[m, 1].astype(F32)
            mine = pl.ds(pl.multiple_of(q * shard, shard), shard)
            ACT[m, q] = jnp.where(H[m, mine].astype(F32) > 0, total, F32(0.0)).astype(BF)
            st[key] = (same(ACT.at[m, q], "y+"), same(ACT.at[m, q], "y-"))
        elif k == 3:
            st[key] = (
                same(ACT.at[m, yi(-1), lo], "y+"),
                same(ACT.at[m, yi(1), hi], "y-"),
            )
        elif k == 4:
            if m == 0:
                load_w1.wait()
            tile = 256

            @pl.loop(0, block // tile)
            def _(n):
                cols = pl.ds(pl.multiple_of(n * tile, tile), tile)
                part = jnp.dot(
                    ACT[m].reshape(tok, hidden_cols), W1[:, cols], preferred_element_type=F32
                )
                N[m, :, :, :, cols] = part.astype(BF).reshape(X, Z, rows, tile)

    def add(index, received):
        N[index] = (N[index].astype(F32) + received.astype(F32)).astype(BF)

    def rs_a(m, k):
        key = ("rsa", m)
        if k > 0:
            wait2(key)
        lo, hi = pl.ds(0, 2), pl.ds(2, 2)
        if k == 0:
            st[key] = (
                send(N.at[m, lo, zi(4), :, A], RA4.at[m, 0], "z+"),
                send(N.at[m, hi, zi(4), :, A], RA4.at[m, 1], "z-"),
            )
        elif k < 4:
            d = 4 - k
            if k == 1:
                add((m, lo, zi(3), slice(None), A), RA4[m, 0])
                add((m, hi, zi(-3), slice(None), A), RA4[m, 1])
            else:
                add((m, slice(None), zi(d), slice(None), A), RA[m, 0, d])
                add((m, slice(None), zi(-d), slice(None), A), RA[m, 1, d])
            st[key] = (
                send(N.at[m, :, zi(d), :, A], RA.at[m, 0, d - 1], "z+"),
                send(N.at[m, :, zi(-d), :, A], RA.at[m, 1, d - 1], "z-"),
            )
        elif k == 4:
            index = (m, slice(None), z, slice(None), A)
            N[index] = (
                N[index].astype(F32) + RA[m, 0, 0].astype(F32) + RA[m, 1, 0].astype(F32)
            ).astype(BF)
            st[key] = (
                send(N.at[m, xi(2), z, :, A], RAX2.at[m], "x+" if m % 2 == 0 else "x-"),
            )
        elif k == 5:
            far = xi(1) if m % 2 == 0 else xi(-1)
            add((m, far, z, slice(None), A), RAX2[m])
            st[key] = (
                send(N.at[m, xi(1), z, :, A], RAX1.at[m, 0], "x+"),
                send(N.at[m, xi(-1), z, :, A], RAX1.at[m, 1], "x-"),
            )
        else:
            index = (m, x, z, slice(None), A)
            N[index] = (
                N[index].astype(F32) + RAX1[m, 0].astype(F32) + RAX1[m, 1].astype(F32)
            ).astype(BF)

    def rs_b(m, k):
        key = ("rsb", m)
        if k > 0:
            wait2(key)
        lo, hi = pl.ds(0, 4), pl.ds(4, 4)
        every = slice(None)
        if k == 0:
            st[key] = (
                send(N.at[m, xi(2), lo, :, B], RB2.at[m, 0], "x+"),
                send(N.at[m, xi(2), hi, :, B], RB2.at[m, 1], "x-"),
            )
        elif k == 1:
            add((m, xi(1), lo, every, B), RB2[m, 0])
            add((m, xi(-1), hi, every, B), RB2[m, 1])
            st[key] = (
                send(N.at[m, xi(1), :, :, B], RB1.at[m, 0], "x+"),
                send(N.at[m, xi(-1), :, :, B], RB1.at[m, 1], "x-"),
            )
        elif k == 2:
            index = (m, x, every, every, B)
            N[index] = (
                N[index].astype(F32) + RB1[m, 0].astype(F32) + RB1[m, 1].astype(F32)
            ).astype(BF)
            st[key] = (
                send(N.at[m, x, zi(4), :, B], RBZ4.at[m], "z+" if m % 2 == 0 else "z-"),
            )
        elif k < 6:
            d = 6 - k
            if k == 3:
                add((m, x, zi(3) if m % 2 == 0 else zi(-3), every, B), RBZ4[m])
            else:
                add((m, x, zi(d), every, B), RBZ[m, 0, d])
                add((m, x, zi(-d), every, B), RBZ[m, 1, d])
            st[key] = (
                send(N.at[m, x, zi(d), :, B], RBZ.at[m, 0, d - 1], "z+"),
                send(N.at[m, x, zi(-d), :, B], RBZ.at[m, 1, d - 1], "z-"),
            )
        else:
            index = (m, x, z, every, B)
            N[index] = (
                N[index].astype(F32) + RBZ[m, 0, 0].astype(F32) + RBZ[m, 1, 0].astype(F32)
            ).astype(BF)

    def weight_grad(j):
        tile = 256
        cols = pl.ds(j * tile, tile)
        left = G[:, :, :, :, cols].reshape(Y * tok, tile)
        part = lax.dot_general(
            left, H[...].reshape(Y * tok, hidden_cols), (((0,), (0,)), ((), ())),
            preferred_element_type=F32,
        )
        WGR[cols] = part.astype(BF)
        c = pltpu.make_async_copy(WGR.at[cols], wg_hbm.at[cols], lsem.at[3 + j])
        c.start()
        outs.append(c)

    outs = []

    def norm_stats():
        values = layer_ref[...].astype(F32)
        center = values - jnp.mean(values, axis=-1, keepdims=True)
        scale = lax.rsqrt(jnp.mean(center * center, axis=-1, keepdims=True) + NORM_EPS)
        xhat[...] = center * scale
        inv[...] = jnp.broadcast_to(scale, inv.shape)

    for c in first:
        c.wait_recv()

    for kind, m, k in ORDER:
        if kind == AG_A:
            ag_a(m, k)
        elif kind == AG_B:
            ag_b(m, k)
        elif kind == YR:
            if m == Y - 1 and k == 4:
                drain()
            y_step(m, k)
        elif kind == RS_A:
            rs_a(m, k)
        elif kind == RS_B:
            rs_b(m, k)
        elif kind == WG:
            weight_grad(m)
        elif kind == HF:
            hidden_step(k)
        else:
            norm_stats()

    last = []
    for d, where in ((1, "y+"), (3, "y-"), (2, "y2")):
        last.append(send(N.at[yi(d), x, z], final.at[q], where))
    final[q] = N[q, x, z]
    for c in outs:
        c.wait()
    for c in last:
        c.wait_recv()

    scale = inv[:, 0:1]
    total = jnp.zeros((rows, 1), F32)
    dotted = jnp.zeros((rows, 1), F32)
    for j in range(Y):
        cols = slice(j * block, (j + 1) * block)
        scaled = final[j].astype(F32) * gain_ref[:, cols]
        total += jnp.sum(scaled, axis=-1, keepdims=True)
        dotted += jnp.sum(scaled * xhat[:, cols], axis=-1, keepdims=True)
    total = total / width
    dotted = dotted / width
    for j in range(Y):
        cols = slice(j * block, (j + 1) * block)
        scaled = final[j].astype(F32) * gain_ref[:, cols]
        bracket = scaled - total - xhat[:, cols] * dotted
        result[:, cols] = (grad_ref[:, cols].astype(F32) + scale * bracket).astype(BF)
    done = send(result, out_hbm, "c")
    done.wait_recv()
    drain()


COPIES = 8 + 3 * 2 + 1 + Y * (11 + 13 + 8 + 13 + 11) + 8


def shards(grad_out, drop_seed, layer_in, ln_gain, pre_act, fc1_weight, fc2_weight):
    rows, width = grad_out.shape[2:]
    tok, hidden = pre_act.shape[2:]
    block = width // Y
    a = (block * 5 // 12) // 128 * 128
    b = block - a
    shard = tok // Y
    vmem = pl.BlockSpec(memory_space=pltpu.VMEM)
    anyspace = pl.BlockSpec(memory_space=pl.ANY)
    arriving, weight_grad = pl.pallas_call(
        functools.partial(kernel, a),
        out_shape=(
            jax.ShapeDtypeStruct((rows, width), BF),
            jax.ShapeDtypeStruct((block, hidden), BF),
        ),
        in_specs=[pl.BlockSpec(memory_space=pltpu.SMEM), vmem, vmem, vmem] + [anyspace] * 3,
        out_specs=(anyspace, anyspace),
        scratch_shapes=[
            pltpu.VMEM((Y, rows, block), BF),
            pltpu.VMEM((Y, X, Z, rows, block), BF),
            pltpu.VMEM((Y, tok, hidden), BF),
            pltpu.VMEM((hidden, block), BF),
            pltpu.VMEM((block, hidden), BF),
            pltpu.VMEM((Y, Y, shard, hidden), BF),
            pltpu.VMEM((Y, 2, shard // 2, hidden), BF),
            pltpu.VMEM((Y, 2, shard, hidden), BF),
            pltpu.VMEM((Y, Y, shard, hidden), BF),
            pltpu.VMEM((Y, X, Z, rows, block), BF),
            pltpu.VMEM((Y, 2, X // 2, rows, a), BF),
            pltpu.VMEM((Y, 2, 3, X, rows, a), BF),
            pltpu.VMEM((Y, rows, a), BF),
            pltpu.VMEM((Y, 2, rows, a), BF),
            pltpu.VMEM((Y, 2, Z // 2, rows, b), BF),
            pltpu.VMEM((Y, 2, Z, rows, b), BF),
            pltpu.VMEM((Y, rows, b), BF),
            pltpu.VMEM((Y, 2, 3, rows, b), BF),
            pltpu.VMEM((block, hidden), BF),
            pltpu.VMEM((rows, width), F32),
            pltpu.VMEM((rows, 128), F32),
            pltpu.VMEM((Y, rows, block), BF),
            pltpu.VMEM((rows, width), BF),
            pltpu.SemaphoreType.DMA((COPIES,)),
            pltpu.SemaphoreType.DMA((COPIES,)),
            pltpu.SemaphoreType.DMA((12,)),
        ],
        compiler_params=pltpu.CompilerParams(
            collective_id=0, has_side_effects=True, vmem_limit_bytes=60 * 1024 * 1024
        ),
    )(
        drop_seed, grad_out[0, 0], layer_in[0, 0], ln_gain,
        pre_act[0, 0], fc1_weight[0], fc2_weight[0],
    )
    return (arriving[None, None], weight_grad[None])


def solution(mesh):
    placed = (
        P("section", "dp", "tensor", None),
        P("section"),
        P("section", "dp", "tensor", None),
        P("section", None),
        P("section", "dp", None, "tensor"),
        P("section", "tensor", "dp"),
        P("section", "dp", "tensor"),
    )
    return jax.shard_map(
        shards,
        mesh=mesh,
        in_specs=placed,
        out_specs=(P("section", "dp", "tensor", None), P("section", "dp", "tensor")),
        check_vma=False,
    )
```

```python
import functools

import jax
import jax.numpy as jnp
from jax import lax
from jax.experimental import pallas as pl
from jax.experimental.pallas import tpu as pltpu
from jax.sharding import PartitionSpec as P

KEEP_SCALE = 1.0 / 0.9
NORM_EPS = 1e-05
MESH = pl.DeviceIdType.MESH
X, Z, Y = 4, 8, 4
BF, F32 = jnp.bfloat16, jnp.float32

AG_A, AG_B, Y_LO, RS_A, RS_B, WG, HF, Y_HI, MM = range(9)


ORDER = (
    (1, 0, 0), (1, 2, 0), (0, 0, 0), (6, 0, 0), (1, 1, 0), (1, 0, 1), (0, 0, 1), (1, 2, 1), (0,
    3, 0), (1, 1, 1), (1, 0, 2), (0, 2, 0), (0, 0, 2), (1, 0, 3), (1, 3, 0), (0, 2, 1), (1, 2,
    2), (0, 0, 3), (0, 3, 1), (0, 2, 2), (1, 0, 4), (0, 0, 4), (0, 2, 3), (1, 2, 3), (1, 1, 2),
    (1, 3, 1), (0, 1, 0), (0, 0, 5), (0, 3, 2), (1, 0, 5), (1, 2, 4), (1, 3, 2), (6, 0, 1), (0,
    2, 4), (0, 1, 1), (0, 0, 6), (1, 0, 6), (2, 0, 0), (7, 0, 0), (1, 3, 3), (6, 0, 2), (2, 0,
    1), (0, 2, 5), (1, 2, 5), (0, 3, 3), (7, 0, 1), (2, 0, 2), (1, 3, 4), (0, 3, 4), (0, 2, 6),
    (1, 2, 6), (2, 2, 0), (7, 0, 2), (0, 1, 2), (7, 2, 0), (2, 2, 1), (0, 3, 5), (2, 0, 3), (1,
    3, 5), (0, 1, 3), (1, 1, 3), (7, 0, 3), (7, 2, 1), (0, 3, 6), (1, 1, 4), (2, 2, 2), (1, 3,
    6), (7, 3, 0), (2, 3, 0), (0, 1, 4), (8, 0, 4), (7, 2, 2), (4, 0, 0), (3, 0, 0), (7, 3, 1),
    (2, 2, 3), (1, 1, 5), (7, 2, 3), (0, 1, 5), (2, 3, 1), (4, 0, 1), (3, 0, 1), (7, 3, 2), (1,
    1, 6), (8, 2, 4), (0, 1, 6), (4, 2, 0), (3, 0, 2), (2, 3, 2), (7, 1, 0), (3, 2, 0), (7, 3,
    3), (2, 1, 0), (2, 3, 3), (4, 0, 2), (4, 2, 1), (7, 1, 1), (2, 1, 1), (8, 3, 4), (4, 3, 0),
    (4, 0, 3), (3, 2, 1), (3, 3, 0), (3, 0, 3), (7, 1, 2), (4, 0, 4), (2, 1, 2), (3, 2, 2), (3,
    3, 1), (4, 3, 1), (7, 1, 3), (3, 0, 4), (2, 1, 3), (4, 2, 2), (3, 2, 3), (6, 0, 3), (8, 1,
    4), (4, 1, 0), (3, 1, 0), (3, 3, 2), (3, 1, 1), (4, 2, 3), (4, 3, 2), (4, 1, 1), (4, 0, 5),
    (3, 3, 3), (3, 1, 2), (6, 0, 4), (5, 1, 0), (5, 2, 0), (3, 2, 4), (4, 2, 4), (4, 3, 3), (5,
    5, 0), (4, 1, 2), (3, 1, 3), (5, 4, 0), (3, 3, 4), (4, 1, 3), (5, 3, 0), (4, 3, 4), (3, 1,
    4), (3, 3, 5), (3, 0, 5), (4, 0, 6), (4, 1, 4), (4, 2, 5), (5, 0, 0), (4, 3, 5), (3, 1, 5),
    (4, 1, 5), (3, 2, 5), (4, 3, 6), (3, 0, 6), (4, 2, 6), (3, 3, 6), (3, 2, 6), (3, 1, 6), (4,
    1, 6),
)


def scramble(hashed):
    hashed = hashed * jnp.int32(739982445)
    hashed = hashed ^ jnp.right_shift(hashed, 15) & jnp.int32(131071)
    hashed = hashed * jnp.int32(695872825)
    hashed = hashed ^ jnp.right_shift(hashed, 13) & jnp.int32(524287)
    return hashed


def kernel(
    cols_a, cut, early, seed_ref, grad_hbm, layer_hbm, gain_hbm, pre_hbm, w1_hbm, w2_hbm,
    final, grad_out, layer_out, gain_out, wg_hbm,
    grad_ref, branch, G, H, W1, W2, PH, RY1A, RY2A, RY1B, RY2B, ACT, N, RA4, RA, RAX2, RAX1, RB2, RB1, RBZ4, RBZ,
    WGR, ssem, rsem, lsem,
):
    s = lax.axis_index("section")
    t = lax.axis_index("tensor")
    q = lax.axis_index("dp")
    x, z = t // Z, t % Z
    rows = grad_ref.shape[0]
    width = grad_ref.shape[1]
    block = width // Y
    hidden_cols = H.shape[-1]
    tok = H.shape[1]
    shard = tok // Y
    half = shard // 2
    A, B = pl.ds(0, cols_a), pl.ds(cols_a, block - cols_a)

    def xi(d):
        return (x + d + X) % X

    def zi(d):
        return (z + d + Z) % Z

    def yi(d):
        return (q + d + Y) % Y

    to = {
        "x+": (s, xi(1) * Z + z, q),
        "x-": (s, xi(-1) * Z + z, q),
        "z+": (s, x * Z + zi(1), q),
        "z-": (s, x * Z + zi(-1), q),
        "y+": (s, t, yi(1)),
        "y-": (s, t, yi(-1)),
        "y2": (s, t, yi(2)),
        "c": (1 - s, t, q),
        "cy+": (1 - s, t, yi(1)),
        "cy-": (1 - s, t, yi(-1)),
        "cy2": (1 - s, t, yi(2)),
    }
    count = [0]
    pending = {}

    def send(*parts, whole=None):
        i = count[0]
        count[0] += 1
        slot = i % SLOTS
        if slot in pending:
            pending.pop(slot).wait_send()

        def copy(src, dst, where):
            return pltpu.make_async_remote_copy(
                src_ref=src, dst_ref=dst, send_sem=ssem.at[slot], recv_sem=rsem.at[i],
                device_id=to[where], device_id_type=MESH,
            )

        for part in parts:
            started = copy(*part)
            started.start()
        pending[slot] = started if whole is None else copy(whole, whole, parts[0][2])
        return (pending[slot],)

    def drain():
        for c in pending.values():
            c.wait_send()
        pending.clear()

    with jax.named_scope("start"):
        barrier = pltpu.get_barrier_semaphore()
        for where in to.values():
            pl.semaphore_signal(barrier, inc=1, device_id=where, device_id_type=MESH)
        load_grad = pltpu.make_async_copy(grad_hbm, grad_ref, lsem.at[9])
        load_grad.start()
        load_pre = pltpu.make_async_copy(pre_hbm, H.at[q], lsem.at[0])
        load_w2 = pltpu.make_async_copy(w2_hbm, W2, lsem.at[1])
        load_w1 = pltpu.make_async_copy(w1_hbm, W1, lsem.at[2])
        load_pre.start()
        load_w2.start()
        load_w1.start()
        load_grad.wait()

        offset = (seed_ref[0] * jnp.int32(131) + q) * jnp.int32(1640531527)
        row_ids = t * rows + lax.broadcasted_iota(jnp.int32, (rows, block), 0)
        col_ids = lax.broadcasted_iota(jnp.int32, (rows, block), 1)
        base = row_ids * jnp.int32(width) + col_ids + offset
        for j in range(Y):
            hashed = scramble(base + jnp.int32(j * block))
            kept = (jnp.right_shift(hashed, 9) & jnp.int32(1023)) < jnp.int32(922)
            factor = jnp.where(kept, F32(KEEP_SCALE), F32(0.0))
            branch[j] = (grad_ref[:, j * block:(j + 1) * block].astype(F32) * factor).astype(BF)
        G[q, x, z] = branch[q]
        load_pre.wait()
        H[q] = jnp.maximum(H[q], jnp.zeros((), BF))

    with jax.named_scope("barrier"):
        pl.semaphore_wait(barrier, len(to))

    first = []
    for d, where in ((1, "y+"), (3, "y-"), (2, "y2")):
        first += send((branch.at[yi(d)], G.at[q, x, z], where))
    shared = []
    for src, dst in ((grad_hbm, grad_out), (layer_hbm, layer_out), (gain_hbm, gain_out)):
        shared += send((src, dst, "c"))

    st = {}

    def hidden_step(k):
        def piece(mb, part, rows_from, rows_count):
            return H.at[mb, pl.ds(pl.multiple_of(part * shard + rows_from, half), rows_count)]

        if k == 0:
            st["h1"] = same(H.at[q], "y+", H.at[q], "y-", whole=H.at[pl.ds(0, 2)])
        elif k == 1:
            wait2("h1")
            st["h2"] = same(
                piece(yi(-1), yi(1), 0, half), "y+", piece(yi(1), yi(-1), half, half), "y-",
                whole=H.at[0, pl.ds(0, shard)],
            )
        elif k == 2:
            wait2("h2")
        elif k == 3:
            st["h3"] = same(
                piece(yi(-1), yi(2), 0, shard), "y+", piece(yi(1), yi(2), 0, shard), "y-",
                whole=H.at[0, pl.ds(0, 2 * shard)],
            ) + same(
                piece(yi(-1), yi(3), 0, half), "y+", piece(yi(1), yi(1), half, half), "y-",
                whole=H.at[0, pl.ds(0, shard)],
            )
        else:
            wait2("h3")

    def wait2(key):
        for c in st.pop(key):
            c.wait_recv()

    def same(ref, where, other=None, other_where=None, whole=None):
        if other is None:
            return send((ref, ref, where))
        return send((ref, ref, where), (other, other, other_where), whole=whole)

    def ag_a(m, k):
        key = ("aga", m)
        if k > 0:
            wait2(key)
        if k == 0:
            own = G.at[m, x, z, :, A]
            st[key] = same(own, "x+", own, "x-", whole=RAX1.at[m])
        elif k == 1:
            if m % 2 == 0:
                st[key] = same(G.at[m, xi(-1), z, :, A], "x+")
            else:
                st[key] = same(G.at[m, xi(1), z, :, A], "x-")
        elif k < 5:
            d = k - 2
            st[key] = same(
                G.at[m, :, zi(-d), :, A], "z+", G.at[m, :, zi(d), :, A], "z-", whole=RA.at[m, :, 0]
            )
        elif k == 5:
            st[key] = same(
                G.at[m, pl.ds(0, 2), zi(-3), :, A], "z+", G.at[m, pl.ds(2, 2), zi(3), :, A], "z-",
                whole=RA4.at[m],
            )

    def ag_b(m, k):
        key = ("agb", m)
        if k > 0:
            wait2(key)
        if k < 3:
            st[key] = same(
                G.at[m, x, zi(-k), :, B], "z+", G.at[m, x, zi(k), :, B], "z-", whole=RBZ.at[m, :, 0]
            )
        elif k == 3:
            if m % 2 == 0:
                st[key] = same(G.at[m, x, zi(-3), :, B], "z+")
            else:
                st[key] = same(G.at[m, x, zi(3), :, B], "z-")
        elif k == 4:
            own = G.at[m, x, :, :, B]
            st[key] = same(own, "x+", own, "x-", whole=RB1.at[m])
        elif k == 5:
            st[key] = same(
                G.at[m, xi(-1), pl.ds(0, 4), :, B], "x+", G.at[m, xi(1), pl.ds(4, 4), :, B], "x-",
                whole=RB2.at[m],
            )

    parts = ((0, cut, RY1A, RY2A), (cut, hidden_cols - cut, RY1B, RY2B))

    def y_step(j, m, k):
        key = ("y", j, m)
        start, size, R1, R2 = parts[j]
        cols = pl.ds(start, size)
        lo, hi = pl.ds(0, half), pl.ds(half, half)
        if k > 0:
            wait2(key)
        if k == 0:
            if m == 0 and j == 0:
                load_w2.wait()
            part = jnp.dot(G[m].reshape(tok, block), W2[:, cols], preferred_element_type=F32)
            PH[m, :, :, cols] = part.astype(BF).reshape(Y, shard, size)
            st[key] = send(
                (PH.at[m, yi(2), lo, cols], R1.at[m, 0], "y+"),
                (PH.at[m, yi(2), hi, cols], R1.at[m, 1], "y-"),
                whole=R1.at[m],
            )
        elif k == 1:
            PH[m, yi(1), lo, cols] = PH[m, yi(1), lo, cols] + R1[m, 0]
            PH[m, yi(-1), hi, cols] = PH[m, yi(-1), hi, cols] + R1[m, 1]
            st[key] = send(
                (PH.at[m, yi(1), :, cols], R2.at[m, 0], "y+"),
                (PH.at[m, yi(-1), :, cols], R2.at[m, 1], "y-"),
                whole=R2.at[m],
            )
        elif k == 2:
            total = PH[m, q, :, cols].astype(F32) + R2[m, 0].astype(F32) + R2[m, 1].astype(F32)
            mine = pl.ds(pl.multiple_of(q * shard, shard), shard)
            ACT[m, q, :, cols] = jnp.where(
                H[m, mine, cols].astype(F32) > 0, total, F32(0.0)
            ).astype(BF)
            own = ACT.at[m, q, :, cols]
            st[key] = same(own, "y+", own, "y-", whole=R2.at[m])
        elif k == 3:
            st[key] = same(
                ACT.at[m, yi(-1), lo, cols], "y+", ACT.at[m, yi(1), hi, cols], "y-", whole=R1.at[m]
            )

    def norm_part(m, cols):
        part = jnp.dot(ACT[m].reshape(tok, hidden_cols), W1[:, cols], preferred_element_type=F32)
        N[m, :, :, :, cols] = part.astype(BF).reshape(X, Z, rows, cols.size)

    def mm_step(m, k):
        if m == 0:
            load_w1.wait()
        wait2(("y", 0, m))
        wait2(("y", 1, m))
        norm_part(m, pl.ds(early, block - early))

    def add(index, received):
        N[index] = N[index] + received

    def rs_a(m, k):
        key = ("rsa", m)
        if k > 0:
            wait2(key)
        lo, hi = pl.ds(0, 2), pl.ds(2, 2)
        if k == 0:
            norm_part(m, pl.ds(0, early))
            st[key] = send(
                (N.at[m, lo, zi(4), :, A], RA4.at[m, 0], "z+"),
                (N.at[m, hi, zi(4), :, A], RA4.at[m, 1], "z-"),
                whole=RA4.at[m],
            )
        elif k < 4:
            d = 4 - k
            if k == 1:
                add((m, lo, zi(3), slice(None), A), RA4[m, 0])
                add((m, hi, zi(-3), slice(None), A), RA4[m, 1])
            else:
                add((m, slice(None), zi(d), slice(None), A), RA[m, 0, d])
                add((m, slice(None), zi(-d), slice(None), A), RA[m, 1, d])
            st[key] = send(
                (N.at[m, :, zi(d), :, A], RA.at[m, 0, d - 1], "z+"),
                (N.at[m, :, zi(-d), :, A], RA.at[m, 1, d - 1], "z-"),
                whole=RA.at[m, :, d - 1],
            )
        elif k == 4:
            index = (m, slice(None), z, slice(None), A)
            N[index] = (
                N[index].astype(F32) + RA[m, 0, 0].astype(F32) + RA[m, 1, 0].astype(F32)
            ).astype(BF)
            st[key] = send((N.at[m, xi(2), z, :, A], RAX2.at[m], "x+" if m % 2 == 0 else "x-"))
        elif k == 5:
            far = xi(1) if m % 2 == 0 else xi(-1)
            add((m, far, z, slice(None), A), RAX2[m])
            st[key] = send(
                (N.at[m, xi(1), z, :, A], RAX1.at[m, 0], "x+"),
                (N.at[m, xi(-1), z, :, A], RAX1.at[m, 1], "x-"),
                whole=RAX1.at[m],
            )
        else:
            index = (m, x, z, slice(None), A)
            N[index] = (
                N[index].astype(F32) + RAX1[m, 0].astype(F32) + RAX1[m, 1].astype(F32)
            ).astype(BF)

    def rs_b(m, k):
        key = ("rsb", m)
        if k > 0:
            wait2(key)
        lo, hi = pl.ds(0, 4), pl.ds(4, 4)
        every = slice(None)
        if k == 0:
            st[key] = send(
                (N.at[m, xi(2), lo, :, B], RB2.at[m, 0], "x+"),
                (N.at[m, xi(2), hi, :, B], RB2.at[m, 1], "x-"),
                whole=RB2.at[m],
            )
        elif k == 1:
            add((m, xi(1), lo, every, B), RB2[m, 0])
            add((m, xi(-1), hi, every, B), RB2[m, 1])
            st[key] = send(
                (N.at[m, xi(1), :, :, B], RB1.at[m, 0], "x+"),
                (N.at[m, xi(-1), :, :, B], RB1.at[m, 1], "x-"),
                whole=RB1.at[m],
            )
        elif k == 2:
            index = (m, x, every, every, B)
            N[index] = (
                N[index].astype(F32) + RB1[m, 0].astype(F32) + RB1[m, 1].astype(F32)
            ).astype(BF)
            st[key] = send((N.at[m, x, zi(4), :, B], RBZ4.at[m], "z+" if m % 2 == 0 else "z-"))
        elif k < 6:
            d = 6 - k
            if k == 3:
                add((m, x, zi(3) if m % 2 == 0 else zi(-3), every, B), RBZ4[m])
            else:
                add((m, x, zi(d), every, B), RBZ[m, 0, d])
                add((m, x, zi(-d), every, B), RBZ[m, 1, d])
            st[key] = send(
                (N.at[m, x, zi(d), :, B], RBZ.at[m, 0, d - 1], "z+"),
                (N.at[m, x, zi(-d), :, B], RBZ.at[m, 1, d - 1], "z-"),
                whole=RBZ.at[m, :, d - 1],
            )
        else:
            index = (m, x, z, every, B)
            N[index] = (
                N[index].astype(F32) + RBZ[m, 0, 0].astype(F32) + RBZ[m, 1, 0].astype(F32)
            ).astype(BF)

    def weight_grad(j):
        tile = 256
        cols = pl.ds(j * tile, tile)
        left = G[:, :, :, :, cols].reshape(Y * tok, tile)
        part = lax.dot_general(
            left, H[...].reshape(Y * tok, hidden_cols), (((0,), (0,)), ((), ())),
            preferred_element_type=F32,
        )
        WGR[cols] = part.astype(BF)
        c = pltpu.make_async_copy(WGR.at[cols], wg_hbm.at[cols], lsem.at[3 + j])
        c.start()
        outs.append(c)

    outs = []

    with jax.named_scope("first"):
        for c in first:
            c.wait_recv()

    steps = {
        AG_A: ag_a, AG_B: ag_b, RS_A: rs_a, RS_B: rs_b, MM: mm_step,
        Y_LO: functools.partial(y_step, 0), Y_HI: functools.partial(y_step, 1),
    }
    for kind, m, k in ORDER:
        if kind == WG:
            weight_grad(m)
        elif kind == HF:
            hidden_step(k)
        else:
            steps[kind](m, k)

    with jax.named_scope("last"):
        last = []
        for d, where in ((1, "cy+"), (3, "cy-"), (2, "cy2"), (0, "c")):
            last += send((N.at[yi(d), x, z], final.at[q], where))
        drain()
        for c in outs:
            c.wait()
        for c in shared:
            c.wait_recv()
        for c in last:
            c.wait_recv()


STRIPS = 8


def norm_back(final, grad, layer, gain, wg_in, out, wg_out, fin, up, lay, gai, res, wg, sems):
    strips = [pl.ds(i * (wg.shape[0] // STRIPS), wg.shape[0] // STRIPS) for i in range(STRIPS)]
    ins = [pltpu.make_async_copy(wg_in.at[r], wg.at[r], sems.at[6 + i]) for i, r in enumerate(strips)]
    outs = [pltpu.make_async_copy(wg.at[r], wg_out.at[r], sems.at[6 + i]) for i, r in enumerate(strips)]
    loads = [
        pltpu.make_async_copy(src, dst, sems.at[1 + i])
        for i, (src, dst) in enumerate(((layer, lay), (final, fin), (gain, gai), (grad, up)))
    ]
    for c in loads:
        c.start()
    for c in ins:
        c.start()
    width = lay.shape[1]
    block = width // Y
    loads[0].wait()
    values = lay[...].astype(F32)
    center = values - jnp.mean(values, axis=-1, keepdims=True)
    scale = lax.rsqrt(jnp.mean(center * center, axis=-1, keepdims=True) + NORM_EPS)
    for c in loads[1:]:
        c.wait()
    for i in range(STRIPS):
        ins[i].wait()
        outs[i].start()
    total = jnp.zeros((lay.shape[0], 1), F32)
    dotted = jnp.zeros((lay.shape[0], 1), F32)
    for j in range(Y):
        cols = slice(j * block, (j + 1) * block)
        scaled = fin[j].astype(F32) * gai[:, cols]
        total += jnp.sum(scaled, axis=-1, keepdims=True)
        dotted += jnp.sum(scaled * (center[:, cols] * scale), axis=-1, keepdims=True)
    total = total / width
    dotted = dotted / width
    for j in range(Y):
        cols = slice(j * block, (j + 1) * block)
        scaled = fin[j].astype(F32) * gai[:, cols]
        bracket = scaled - total - (center[:, cols] * scale) * dotted
        res[:, cols] = (up[:, cols].astype(F32) + scale * bracket).astype(BF)
    store = pltpu.make_async_copy(res, out, sems.at[5])
    store.start()
    store.wait()
    for c in outs:
        c.wait()


SLOTS = 48
COPIES = 3 + 3 + 4 + Y * 32 + 4


def shards(grad_out, drop_seed, layer_in, ln_gain, pre_act, fc1_weight, fc2_weight):
    rows, width = grad_out.shape[2:]
    tok, hidden = pre_act.shape[2:]
    block = width // Y
    a = (block * 5 // 12) // 128 * 128
    b = block - a
    shard = tok // Y
    cut = hidden // 3
    early = block // 3
    anyspace = pl.BlockSpec(memory_space=pl.ANY)
    final, grad_there, layer_there, gain_there, weight_grad = pl.pallas_call(
        functools.partial(kernel, a, cut, early),
        out_shape=(
            jax.ShapeDtypeStruct((Y, rows, block), BF),
            jax.ShapeDtypeStruct((rows, width), BF),
            jax.ShapeDtypeStruct((rows, width), BF),
            jax.ShapeDtypeStruct((1, width), F32),
            jax.ShapeDtypeStruct((block, hidden), BF),
        ),
        in_specs=[pl.BlockSpec(memory_space=pltpu.SMEM)] + [anyspace] * 6,
        out_specs=(anyspace,) * 5,
        scratch_shapes=[
            pltpu.VMEM((rows, width), BF),
            pltpu.VMEM((Y, rows, block), BF),
            pltpu.VMEM((Y, X, Z, rows, block), BF),
            pltpu.VMEM((Y, tok, hidden), BF),
            pltpu.VMEM((hidden, block), BF),
            pltpu.VMEM((block, hidden), BF),
            pltpu.VMEM((Y, Y, shard, hidden), BF),
            pltpu.VMEM((Y, 2, shard // 2, cut), BF),
            pltpu.VMEM((Y, 2, shard, cut), BF),
            pltpu.VMEM((Y, 2, shard // 2, hidden - cut), BF),
            pltpu.VMEM((Y, 2, shard, hidden - cut), BF),
            pltpu.VMEM((Y, Y, shard, hidden), BF),
            pltpu.VMEM((Y, X, Z, rows, block), BF),
            pltpu.VMEM((Y, 2, X // 2, rows, a), BF),
            pltpu.VMEM((Y, 2, 3, X, rows, a), BF),
            pltpu.VMEM((Y, rows, a), BF),
            pltpu.VMEM((Y, 2, rows, a), BF),
            pltpu.VMEM((Y, 2, Z // 2, rows, b), BF),
            pltpu.VMEM((Y, 2, Z, rows, b), BF),
            pltpu.VMEM((Y, rows, b), BF),
            pltpu.VMEM((Y, 2, 3, rows, b), BF),
            pltpu.VMEM((block, hidden), BF),
            pltpu.SemaphoreType.DMA((SLOTS,)),
            pltpu.SemaphoreType.DMA((COPIES,)),
            pltpu.SemaphoreType.DMA((10,)),
        ],
        compiler_params=pltpu.CompilerParams(
            collective_id=0, has_side_effects=True, vmem_limit_bytes=60 * 1024 * 1024
        ),
    )(
        drop_seed, grad_out[0, 0], layer_in[0, 0], ln_gain,
        pre_act[0, 0], fc1_weight[0], fc2_weight[0],
    )
    arriving, weight_grad = pl.pallas_call(
        norm_back,
        out_shape=(
            jax.ShapeDtypeStruct((rows, width), BF),
            jax.ShapeDtypeStruct((block, hidden), BF),
        ),
        in_specs=[anyspace] * 5,
        out_specs=(anyspace,) * 2,
        scratch_shapes=[
            pltpu.VMEM((Y, rows, block), BF),
            pltpu.VMEM((rows, width), BF),
            pltpu.VMEM((rows, width), BF),
            pltpu.VMEM((1, width), F32),
            pltpu.VMEM((rows, width), BF),
            pltpu.VMEM((block, hidden), BF),
            pltpu.SemaphoreType.DMA((6 + STRIPS,)),
        ],
    )(final, grad_there, layer_there, gain_there, weight_grad)
    return (arriving[None, None], weight_grad[None])


def solution(mesh):
    placed = (
        P("section", "dp", "tensor", None),
        P("section"),
        P("section", "dp", "tensor", None),
        P("section", None),
        P("section", "dp", None, "tensor"),
        P("section", "tensor", "dp"),
        P("section", "dp", "tensor"),
    )
    return jax.shard_map(
        shards,
        mesh=mesh,
        in_specs=placed,
        out_specs=(P("section", "dp", "tensor", None), P("section", "dp", "tensor")),
        check_vma=False,
    )
```

```python
import functools

import jax
import jax.numpy as jnp
from jax import lax
from jax.experimental import pallas as pl
from jax.experimental.pallas import tpu as pltpu
from jax.sharding import PartitionSpec as P

KEEP_SCALE = 1.0 / 0.9
NORM_EPS = 1e-05
MESH = pl.DeviceIdType.MESH
X, Z, Y = 4, 8, 4
BF, F32 = jnp.bfloat16, jnp.float32

AG_A, AG_B, Y_LO, RS_A, RS_B, WG, HF, Y_HI, MM = range(9)


GATHER_DIRECT = (0,)
SCATTER_DIRECT = (3,)

ORDER = (
    (6, 0, 0), (1, 2, 0), (0, 2, 0), (0, 0, 0), (1, 0, 0), (0, 2, 1), (1, 2, 1), (0, 0, 2), (0,
    1, 0), (1, 1, 0), (0, 3, 0), (1, 3, 0), (1, 2, 2), (0, 1, 1), (0, 2, 2), (1, 3, 1), (1, 2,
    3), (0, 0, 3), (1, 0, 4), (0, 2, 3), (1, 1, 1), (1, 2, 4), (0, 0, 4), (6, 0, 1), (0, 3, 1),
    (0, 2, 4), (1, 0, 5), (6, 0, 3), (1, 3, 2), (0, 0, 5), (1, 2, 5), (1, 1, 2), (0, 2, 5), (0,
    1, 2), (1, 0, 6), (0, 0, 6), (2, 0, 0), (0, 3, 2), (1, 1, 3), (7, 0, 0), (0, 2, 6), (6, 0,
    2), (1, 2, 6), (7, 2, 0), (0, 1, 3), (2, 0, 1), (1, 3, 3), (2, 2, 0), (6, 0, 4), (7, 0, 1),
    (5, 2, 4), (7, 2, 1), (1, 1, 4), (0, 1, 4), (2, 2, 1), (1, 3, 4), (0, 3, 3), (7, 0, 2), (2,
    0, 2), (0, 1, 5), (0, 3, 4), (1, 1, 5), (2, 2, 2), (1, 3, 5), (7, 0, 3), (7, 2, 2), (5, 2,
    0), (5, 2, 3), (0, 1, 6), (2, 0, 3), (1, 1, 6), (7, 1, 0), (2, 1, 0), (0, 3, 5), (5, 0, 0),
    (7, 2, 3), (2, 2, 3), (0, 3, 6), (8, 0, 4), (4, 0, 0), (7, 1, 1), (3, 0, 0), (1, 3, 6), (7,
    3, 0), (8, 2, 4), (4, 2, 0), (2, 1, 1), (3, 2, 0), (2, 3, 0), (4, 0, 1), (7, 1, 2), (3, 0,
    1), (3, 2, 1), (2, 1, 2), (5, 3, 0), (7, 3, 1), (3, 0, 2), (5, 2, 2), (2, 3, 1), (4, 2, 1),
    (5, 2, 5), (5, 1, 4), (5, 1, 1), (2, 1, 3), (3, 2, 2), (7, 1, 3), (5, 3, 3), (4, 0, 2), (7,
    3, 2), (3, 0, 3), (5, 0, 1), (5, 0, 3), (5, 1, 2), (4, 2, 2), (2, 3, 2), (3, 2, 3), (8, 1,
    4), (4, 1, 0), (4, 0, 3), (3, 1, 0), (5, 2, 1), (5, 0, 2), (4, 2, 3), (7, 3, 3), (2, 3, 3),
    (3, 1, 1), (4, 1, 1), (3, 0, 4), (4, 2, 4), (4, 0, 4), (8, 3, 4), (3, 3, 0), (4, 3, 0), (3,
    1, 2), (5, 3, 1), (4, 1, 2), (3, 3, 1), (5, 1, 5), (3, 2, 4), (5, 0, 4), (3, 1, 3), (5, 1,
    0), (4, 3, 1), (3, 2, 5), (3, 0, 5), (4, 1, 3), (5, 0, 5), (3, 3, 2), (4, 0, 5), (5, 1, 3),
    (4, 1, 4), (4, 2, 5), (3, 3, 3), (4, 3, 2), (5, 3, 5), (3, 1, 4), (3, 1, 5), (3, 3, 4), (3,
    0, 6), (4, 0, 6), (4, 1, 5), (5, 3, 2), (5, 3, 4), (3, 3, 6), (3, 1, 6), (4, 2, 6), (4, 3,
    6), (3, 2, 6), (4, 1, 6),
)


def scramble(hashed):
    hashed = hashed * jnp.int32(739982445)
    hashed = hashed ^ jnp.right_shift(hashed, 15) & jnp.int32(131071)
    hashed = hashed * jnp.int32(695872825)
    hashed = hashed ^ jnp.right_shift(hashed, 13) & jnp.int32(524287)
    return hashed


def kernel(
    cols_a, cut, early, seed_ref, grad_hbm, layer_hbm, gain_hbm, pre_hbm, w1_hbm, w2_hbm,
    final, grad_out, layer_out, gain_out, wg_hbm,
    grad_ref, branch, G, H, W1, W2, PH, RY1A, RY2A, RY1B, RY2B, ACT, N, RA4, RA, RAX2, RAX1, RB2, RB1, RBZ4, RBZ,
    WACC, WGR, ssem, rsem, lsem,
):
    s = lax.axis_index("section")
    t = lax.axis_index("tensor")
    q = lax.axis_index("dp")
    x, z = t // Z, t % Z
    rows = grad_ref.shape[0]
    width = grad_ref.shape[1]
    block = width // Y
    hidden_cols = H.shape[-1]
    tok = H.shape[1]
    shard = tok // Y
    half = shard // 2
    A, B = pl.ds(0, cols_a), pl.ds(cols_a, block - cols_a)

    def xi(d):
        return (x + d + X) % X

    def zi(d):
        return (z + d + Z) % Z

    def yi(d):
        return (q + d + Y) % Y

    to = {
        "x+": (s, xi(1) * Z + z, q),
        "x-": (s, xi(-1) * Z + z, q),
        "z+": (s, x * Z + zi(1), q),
        "z-": (s, x * Z + zi(-1), q),
        "y+": (s, t, yi(1)),
        "y-": (s, t, yi(-1)),
        "y2": (s, t, yi(2)),
        "x2": (s, xi(2) * Z + z, q),
        "z+2": (s, x * Z + zi(2), q),
        "z-2": (s, x * Z + zi(-2), q),
        "z+3": (s, x * Z + zi(3), q),
        "z-3": (s, x * Z + zi(-3), q),
        "z4": (s, x * Z + zi(4), q),
        "c": (1 - s, t, q),
        "cy+": (1 - s, t, yi(1)),
        "cy-": (1 - s, t, yi(-1)),
        "cy2": (1 - s, t, yi(2)),
    }
    tile = 256
    count = [0]
    pending = {}

    def send(*parts, whole=None):
        i = count[0]
        count[0] += 1
        slot = i % SLOTS
        if slot in pending:
            pending.pop(slot).wait_send()

        def copy(src, dst, where):
            return pltpu.make_async_remote_copy(
                src_ref=src, dst_ref=dst, send_sem=ssem.at[slot], recv_sem=rsem.at[i],
                device_id=to[where], device_id_type=MESH,
            )

        for part in parts:
            started = copy(*part)
            started.start()
        pending[slot] = started if whole is None else copy(whole, whole, parts[0][2])
        return (pending[slot],)

    def drain():
        for c in pending.values():
            c.wait_send()
        pending.clear()

    with jax.named_scope("start"):
        barrier = pltpu.get_barrier_semaphore()
        for where in to.values():
            pl.semaphore_signal(barrier, inc=1, device_id=where, device_id_type=MESH)
        load_grad = pltpu.make_async_copy(grad_hbm, grad_ref, lsem.at[9])
        load_grad.start()
        load_pre = pltpu.make_async_copy(pre_hbm, H.at[q], lsem.at[0])
        load_w2 = pltpu.make_async_copy(w2_hbm, W2, lsem.at[1])
        load_w1 = pltpu.make_async_copy(w1_hbm, W1, lsem.at[2])
        load_pre.start()
        load_w2.start()
        load_w1.start()
        load_grad.wait()

        offset = (seed_ref[0] * jnp.int32(131) + q) * jnp.int32(1640531527)
        row_ids = t * rows + lax.broadcasted_iota(jnp.int32, (rows, block), 0)
        col_ids = lax.broadcasted_iota(jnp.int32, (rows, block), 1)
        base = row_ids * jnp.int32(width) + col_ids + offset
        for j in range(Y):
            hashed = scramble(base + jnp.int32(j * block))
            kept = (jnp.right_shift(hashed, 9) & jnp.int32(1023)) < jnp.int32(922)
            factor = jnp.where(kept, F32(KEEP_SCALE), F32(0.0))
            branch[j] = (grad_ref[:, j * block:(j + 1) * block].astype(F32) * factor).astype(BF)
        G[q, x, z] = branch[q]
        load_pre.wait()
        H[q] = jnp.maximum(H[q], jnp.zeros((), BF))

    with jax.named_scope("barrier"):
        pl.semaphore_wait(barrier, len(to))

    first = []
    for d, where in ((1, "y+"), (3, "y-"), (2, "y2")):
        first += send((branch.at[yi(d)], G.at[q, x, z], where))
    shared = []
    for src, dst in ((grad_hbm, grad_out), (layer_hbm, layer_out), (gain_hbm, gain_out)):
        shared += send((src, dst, "c"))

    st = {}

    def hidden_step(k):
        def piece(mb, part, rows_from, rows_count):
            return H.at[mb, pl.ds(pl.multiple_of(part * shard + rows_from, half), rows_count)]

        if k == 0:
            st["h1"] = same(H.at[q], "y+", H.at[q], "y-", whole=H.at[pl.ds(0, 2)])
        elif k == 1:
            wait2("h1")
            st["h2"] = same(
                piece(yi(-1), yi(1), 0, half), "y+", piece(yi(1), yi(-1), half, half), "y-",
                whole=H.at[0, pl.ds(0, shard)],
            )
        elif k == 2:
            wait2("h2")
        elif k == 3:
            st["h3"] = same(
                piece(yi(-1), yi(2), 0, shard), "y+", piece(yi(1), yi(2), 0, shard), "y-",
                whole=H.at[0, pl.ds(0, 2 * shard)],
            ) + same(
                piece(yi(-1), yi(3), 0, half), "y+", piece(yi(1), yi(1), half, half), "y-",
                whole=H.at[0, pl.ds(0, shard)],
            )
        else:
            wait2("h3")

    def wait2(key):
        for c in st.pop(key):
            c.wait_recv()

    def same(ref, where, other=None, other_where=None, whole=None):
        if other is None:
            return send((ref, ref, where))
        return send((ref, ref, where), (other, other, other_where), whole=whole)

    def ag_a(m, k):
        key = ("aga", m)
        if k > 0:
            wait2(key)
        if k == 0:
            own = G.at[m, x, z, :, A]
            st[key] = same(own, "x+", own, "x-", whole=RAX1.at[m])
            if m in GATHER_DIRECT:
                st[key] += same(own, "x2")
        elif k == 1:
            if m % 2 == 0:
                st[key] = same(G.at[m, xi(-1), z, :, A], "x+")
            else:
                st[key] = same(G.at[m, xi(1), z, :, A], "x-")
        elif k < 5:
            d = k - 2
            st[key] = same(
                G.at[m, :, zi(-d), :, A], "z+", G.at[m, :, zi(d), :, A], "z-", whole=RA.at[m, :, 0]
            )
        elif k == 5:
            st[key] = same(
                G.at[m, pl.ds(0, 2), zi(-3), :, A], "z+", G.at[m, pl.ds(2, 2), zi(3), :, A], "z-",
                whole=RA4.at[m],
            )

    def ag_b(m, k):
        key = ("agb", m)
        if k > 0:
            wait2(key)
        if m in GATHER_DIRECT and k == 0:
            own = G.at[m, x, z, :, B]
            st[key] = same(own, "z+", own, "z-", whole=RBZ.at[m, :, 0])
            st[key] += same(own, "z+2", own, "z-2", whole=RBZ.at[m, :, 0])
            st[key] += same(own, "z+3", own, "z-3", whole=RBZ.at[m, :, 0])
            st[key] += same(own, "z4")
        elif k < 3:
            st[key] = same(
                G.at[m, x, zi(-k), :, B], "z+", G.at[m, x, zi(k), :, B], "z-", whole=RBZ.at[m, :, 0]
            )
        elif k == 3:
            if m % 2 == 0:
                st[key] = same(G.at[m, x, zi(-3), :, B], "z+")
            else:
                st[key] = same(G.at[m, x, zi(3), :, B], "z-")
        elif k == 4:
            own = G.at[m, x, :, :, B]
            st[key] = same(own, "x+", own, "x-", whole=RB1.at[m])
        elif k == 5:
            st[key] = same(
                G.at[m, xi(-1), pl.ds(0, 4), :, B], "x+", G.at[m, xi(1), pl.ds(4, 4), :, B], "x-",
                whole=RB2.at[m],
            )

    parts = ((0, cut, RY1A, RY2A), (cut, hidden_cols - cut, RY1B, RY2B))

    def y_step(j, m, k):
        key = ("y", j, m)
        start, size, R1, R2 = parts[j]
        cols = pl.ds(start, size)
        lo, hi = pl.ds(0, half), pl.ds(half, half)
        if k > 0:
            wait2(key)
        if k == 0:
            if m == 0 and j == 0:
                load_w2.wait()
            part = jnp.dot(G[m].reshape(tok, block), W2[:, cols], preferred_element_type=F32)
            PH[m, :, :, cols] = part.astype(BF).reshape(Y, shard, size)
            st[key] = send(
                (PH.at[m, yi(2), lo, cols], R1.at[m, 0], "y+"),
                (PH.at[m, yi(2), hi, cols], R1.at[m, 1], "y-"),
                whole=R1.at[m],
            )
        elif k == 1:
            PH[m, yi(1), lo, cols] = PH[m, yi(1), lo, cols] + R1[m, 0]
            PH[m, yi(-1), hi, cols] = PH[m, yi(-1), hi, cols] + R1[m, 1]
            st[key] = send(
                (PH.at[m, yi(1), :, cols], R2.at[m, 0], "y+"),
                (PH.at[m, yi(-1), :, cols], R2.at[m, 1], "y-"),
                whole=R2.at[m],
            )
        elif k == 2:
            total = PH[m, q, :, cols].astype(F32) + R2[m, 0].astype(F32) + R2[m, 1].astype(F32)
            mine = pl.ds(pl.multiple_of(q * shard, shard), shard)
            ACT[m, q, :, cols] = jnp.where(
                H[m, mine, cols].astype(F32) > 0, total, F32(0.0)
            ).astype(BF)
            own = ACT.at[m, q, :, cols]
            st[key] = same(own, "y+", own, "y-", whole=R2.at[m])
        elif k == 3:
            st[key] = same(
                ACT.at[m, yi(-1), lo, cols], "y+", ACT.at[m, yi(1), hi, cols], "y-", whole=R1.at[m]
            )

    def norm_part(m, cols):
        part = jnp.dot(ACT[m].reshape(tok, hidden_cols), W1[:, cols], preferred_element_type=F32)
        N[m, :, :, :, cols] = part.astype(BF).reshape(X, Z, rows, cols.size)

    def mm_step(m, k):
        if m == 0:
            load_w1.wait()
        wait2(("y", 0, m))
        wait2(("y", 1, m))
        norm_part(m, pl.ds(early, block - early))

    def add(index, received):
        N[index] = N[index] + received

    def rs_a(m, k):
        key = ("rsa", m)
        if k > 0:
            wait2(key)
        lo, hi = pl.ds(0, 2), pl.ds(2, 2)
        if k == 0:
            norm_part(m, pl.ds(0, early))
            st[key] = send(
                (N.at[m, lo, zi(4), :, A], RA4.at[m, 0], "z+"),
                (N.at[m, hi, zi(4), :, A], RA4.at[m, 1], "z-"),
                whole=RA4.at[m],
            )
        elif k < 4:
            d = 4 - k
            if k == 1:
                add((m, lo, zi(3), slice(None), A), RA4[m, 0])
                add((m, hi, zi(-3), slice(None), A), RA4[m, 1])
            else:
                add((m, slice(None), zi(d), slice(None), A), RA[m, 0, d])
                add((m, slice(None), zi(-d), slice(None), A), RA[m, 1, d])
            st[key] = send(
                (N.at[m, :, zi(d), :, A], RA.at[m, 0, d - 1], "z+"),
                (N.at[m, :, zi(-d), :, A], RA.at[m, 1, d - 1], "z-"),
                whole=RA.at[m, :, d - 1],
            )
        elif k == 4:
            index = (m, slice(None), z, slice(None), A)
            N[index] = (
                N[index].astype(F32) + RA[m, 0, 0].astype(F32) + RA[m, 1, 0].astype(F32)
            ).astype(BF)
            if m in SCATTER_DIRECT:
                st[key] = send(
                    (N.at[m, xi(1), z, :, A], RAX1.at[m, 0], "x+"),
                    (N.at[m, xi(-1), z, :, A], RAX1.at[m, 1], "x-"),
                    whole=RAX1.at[m],
                ) + send((N.at[m, xi(2), z, :, A], RAX2.at[m], "x2"))
            else:
                st[key] = send(
                    (N.at[m, xi(2), z, :, A], RAX2.at[m], "x+" if m % 2 == 0 else "x-")
                )
        elif k == 5:
            far = xi(1) if m % 2 == 0 else xi(-1)
            add((m, far, z, slice(None), A), RAX2[m])
            st[key] = send(
                (N.at[m, xi(1), z, :, A], RAX1.at[m, 0], "x+"),
                (N.at[m, xi(-1), z, :, A], RAX1.at[m, 1], "x-"),
                whole=RAX1.at[m],
            )
        else:
            index = (m, x, z, slice(None), A)
            total = N[index].astype(F32) + RAX1[m, 0].astype(F32) + RAX1[m, 1].astype(F32)
            if m in SCATTER_DIRECT:
                total += RAX2[m].astype(F32)
            N[index] = total.astype(BF)

    def rs_b(m, k):
        key = ("rsb", m)
        if k > 0:
            wait2(key)
        lo, hi = pl.ds(0, 4), pl.ds(4, 4)
        every = slice(None)
        if k == 0:
            st[key] = send(
                (N.at[m, xi(2), lo, :, B], RB2.at[m, 0], "x+"),
                (N.at[m, xi(2), hi, :, B], RB2.at[m, 1], "x-"),
                whole=RB2.at[m],
            )
        elif k == 1:
            add((m, xi(1), lo, every, B), RB2[m, 0])
            add((m, xi(-1), hi, every, B), RB2[m, 1])
            st[key] = send(
                (N.at[m, xi(1), :, :, B], RB1.at[m, 0], "x+"),
                (N.at[m, xi(-1), :, :, B], RB1.at[m, 1], "x-"),
                whole=RB1.at[m],
            )
        elif k == 2:
            index = (m, x, every, every, B)
            N[index] = (
                N[index].astype(F32) + RB1[m, 0].astype(F32) + RB1[m, 1].astype(F32)
            ).astype(BF)
            if m in SCATTER_DIRECT:
                st[key] = ()
                for d, up, down in ((1, "z+", "z-"), (2, "z+2", "z-2"), (3, "z+3", "z-3")):
                    st[key] += send(
                        (N.at[m, x, zi(d), :, B], RBZ.at[m, 0, d - 1], up),
                        (N.at[m, x, zi(-d), :, B], RBZ.at[m, 1, d - 1], down),
                        whole=RBZ.at[m, :, d - 1],
                    )
                st[key] += send((N.at[m, x, zi(4), :, B], RBZ4.at[m], "z4"))
            else:
                st[key] = send(
                    (N.at[m, x, zi(4), :, B], RBZ4.at[m], "z+" if m % 2 == 0 else "z-")
                )
        elif k < 6:
            d = 6 - k
            if k == 3:
                add((m, x, zi(3) if m % 2 == 0 else zi(-3), every, B), RBZ4[m])
            else:
                add((m, x, zi(d), every, B), RBZ[m, 0, d])
                add((m, x, zi(-d), every, B), RBZ[m, 1, d])
            st[key] = send(
                (N.at[m, x, zi(d), :, B], RBZ.at[m, 0, d - 1], "z+"),
                (N.at[m, x, zi(-d), :, B], RBZ.at[m, 1, d - 1], "z-"),
                whole=RBZ.at[m, :, d - 1],
            )
        else:
            index = (m, x, z, every, B)
            total = N[index].astype(F32) + RBZ[m, 0, 0].astype(F32) + RBZ[m, 1, 0].astype(F32)
            if m in SCATTER_DIRECT:
                total += RBZ4[m].astype(F32)
                for d in (1, 2):
                    total += RBZ[m, 0, d].astype(F32) + RBZ[m, 1, d].astype(F32)
            N[index] = total.astype(BF)

    taken = [0] * (block // tile)

    def weight_grad(m, j):
        cols = pl.ds(j * tile, tile)
        part = lax.dot_general(
            G[m, :, :, :, cols].reshape(tok, tile), H[m], (((0,), (0,)), ((), ())),
            preferred_element_type=F32,
        )
        taken[j] += 1
        if taken[j] == 1:
            WACC[cols] = part
        elif taken[j] < Y:
            WACC[cols] += part
        else:
            WGR[cols] = (WACC[cols] + part).astype(BF)
            c = pltpu.make_async_copy(WGR.at[cols], wg_hbm.at[cols], lsem.at[3 + j])
            c.start()
            outs.append(c)

    outs = []

    with jax.named_scope("first"):
        for c in first:
            c.wait_recv()

    steps = {
        AG_A: ag_a, AG_B: ag_b, RS_A: rs_a, RS_B: rs_b, MM: mm_step,
        Y_LO: functools.partial(y_step, 0), Y_HI: functools.partial(y_step, 1),
    }
    for kind, m, k in ORDER:
        if kind == WG:
            weight_grad(m, k)
        elif kind == HF:
            hidden_step(k)
        else:
            steps[kind](m, k)

    with jax.named_scope("last"):
        last = []
        for d, where in ((1, "cy+"), (3, "cy-"), (2, "cy2"), (0, "c")):
            last += send((N.at[yi(d), x, z], final.at[q], where))
        drain()
        for c in outs:
            c.wait()
        for c in shared:
            c.wait_recv()
        for c in last:
            c.wait_recv()


STRIPS = 8


def norm_back(final, grad, layer, gain, wg_in, out, wg_out, fin, up, lay, gai, res, wg, sems):
    strips = [pl.ds(i * (wg.shape[0] // STRIPS), wg.shape[0] // STRIPS) for i in range(STRIPS)]
    ins = [pltpu.make_async_copy(wg_in.at[r], wg.at[r], sems.at[6 + i]) for i, r in enumerate(strips)]
    outs = [pltpu.make_async_copy(wg.at[r], wg_out.at[r], sems.at[6 + i]) for i, r in enumerate(strips)]
    loads = [
        pltpu.make_async_copy(src, dst, sems.at[1 + i])
        for i, (src, dst) in enumerate(((layer, lay), (final, fin), (gain, gai), (grad, up)))
    ]
    for c in loads:
        c.start()
    for c in ins:
        c.start()
    width = lay.shape[1]
    block = width // Y
    loads[0].wait()
    values = lay[...].astype(F32)
    center = values - jnp.mean(values, axis=-1, keepdims=True)
    scale = lax.rsqrt(jnp.mean(center * center, axis=-1, keepdims=True) + NORM_EPS)
    for c in loads[1:]:
        c.wait()
    for i in range(STRIPS):
        ins[i].wait()
        outs[i].start()
    total = jnp.zeros((lay.shape[0], 1), F32)
    dotted = jnp.zeros((lay.shape[0], 1), F32)
    for j in range(Y):
        cols = slice(j * block, (j + 1) * block)
        scaled = fin[j].astype(F32) * gai[:, cols]
        total += jnp.sum(scaled, axis=-1, keepdims=True)
        dotted += jnp.sum(scaled * (center[:, cols] * scale), axis=-1, keepdims=True)
    total = total / width
    dotted = dotted / width
    for j in range(Y):
        cols = slice(j * block, (j + 1) * block)
        scaled = fin[j].astype(F32) * gai[:, cols]
        bracket = scaled - total - (center[:, cols] * scale) * dotted
        res[:, cols] = (up[:, cols].astype(F32) + scale * bracket).astype(BF)
    store = pltpu.make_async_copy(res, out, sems.at[5])
    store.start()
    store.wait()
    for c in outs:
        c.wait()


SPLIT = 768
SLOTS = 48
COPIES = 3 + 3 + 4 + Y * 32 + 4


def shards(grad_out, drop_seed, layer_in, ln_gain, pre_act, fc1_weight, fc2_weight):
    rows, width = grad_out.shape[2:]
    tok, hidden = pre_act.shape[2:]
    block = width // Y
    a = SPLIT
    b = block - a
    shard = tok // Y
    cut = hidden // 3
    early = block // 3
    anyspace = pl.BlockSpec(memory_space=pl.ANY)
    final, grad_there, layer_there, gain_there, weight_grad = pl.pallas_call(
        functools.partial(kernel, a, cut, early),
        out_shape=(
            jax.ShapeDtypeStruct((Y, rows, block), BF),
            jax.ShapeDtypeStruct((rows, width), BF),
            jax.ShapeDtypeStruct((rows, width), BF),
            jax.ShapeDtypeStruct((1, width), F32),
            jax.ShapeDtypeStruct((block, hidden), BF),
        ),
        in_specs=[pl.BlockSpec(memory_space=pltpu.SMEM)] + [anyspace] * 6,
        out_specs=(anyspace,) * 5,
        scratch_shapes=[
            pltpu.VMEM((rows, width), BF),
            pltpu.VMEM((Y, rows, block), BF),
            pltpu.VMEM((Y, X, Z, rows, block), BF),
            pltpu.VMEM((Y, tok, hidden), BF),
            pltpu.VMEM((hidden, block), BF),
            pltpu.VMEM((block, hidden), BF),
            pltpu.VMEM((Y, Y, shard, hidden), BF),
            pltpu.VMEM((Y, 2, shard // 2, cut), BF),
            pltpu.VMEM((Y, 2, shard, cut), BF),
            pltpu.VMEM((Y, 2, shard // 2, hidden - cut), BF),
            pltpu.VMEM((Y, 2, shard, hidden - cut), BF),
            pltpu.VMEM((Y, Y, shard, hidden), BF),
            pltpu.VMEM((Y, X, Z, rows, block), BF),
            pltpu.VMEM((Y, 2, X // 2, rows, a), BF),
            pltpu.VMEM((Y, 2, 3, X, rows, a), BF),
            pltpu.VMEM((Y, rows, a), BF),
            pltpu.VMEM((Y, 2, rows, a), BF),
            pltpu.VMEM((Y, 2, Z // 2, rows, b), BF),
            pltpu.VMEM((Y, 2, Z, rows, b), BF),
            pltpu.VMEM((Y, rows, b), BF),
            pltpu.VMEM((Y, 2, 3, rows, b), BF),
            pltpu.VMEM((block, hidden), F32),
            pltpu.VMEM((block, hidden), BF),
            pltpu.SemaphoreType.DMA((SLOTS,)),
            pltpu.SemaphoreType.DMA((COPIES,)),
            pltpu.SemaphoreType.DMA((10,)),
        ],
        compiler_params=pltpu.CompilerParams(
            collective_id=0, has_side_effects=True, vmem_limit_bytes=60 * 1024 * 1024
        ),
    )(
        drop_seed, grad_out[0, 0], layer_in[0, 0], ln_gain,
        pre_act[0, 0], fc1_weight[0], fc2_weight[0],
    )
    arriving, weight_grad = pl.pallas_call(
        norm_back,
        out_shape=(
            jax.ShapeDtypeStruct((rows, width), BF),
            jax.ShapeDtypeStruct((block, hidden), BF),
        ),
        in_specs=[anyspace] * 5,
        out_specs=(anyspace,) * 2,
        scratch_shapes=[
            pltpu.VMEM((Y, rows, block), BF),
            pltpu.VMEM((rows, width), BF),
            pltpu.VMEM((rows, width), BF),
            pltpu.VMEM((1, width), F32),
            pltpu.VMEM((rows, width), BF),
            pltpu.VMEM((block, hidden), BF),
            pltpu.SemaphoreType.DMA((6 + STRIPS,)),
        ],
    )(final, grad_there, layer_there, gain_there, weight_grad)
    return (arriving[None, None], weight_grad[None])


def solution(mesh):
    placed = (
        P("section", "dp", "tensor", None),
        P("section"),
        P("section", "dp", "tensor", None),
        P("section", None),
        P("section", "dp", None, "tensor"),
        P("section", "tensor", "dp"),
        P("section", "dp", "tensor"),
    )
    return jax.shard_map(
        shards,
        mesh=mesh,
        in_specs=placed,
        out_specs=(P("section", "dp", "tensor", None), P("section", "dp", "tensor")),
        check_vma=False,
    )
```

```python
import functools

import jax
import jax.numpy as jnp
from jax import lax
from jax.experimental import pallas as pl
from jax.experimental.pallas import tpu as pltpu
from jax.sharding import PartitionSpec as P

KEEP_SCALE = 1.0 / 0.9
NORM_EPS = 1e-05
MESH = pl.DeviceIdType.MESH
X, Z, Y = 4, 8, 4
BF, F32 = jnp.bfloat16, jnp.float32

AG_A, AG_B, Y_LO, RS_A, RS_B, WG, HF, Y_HI, MM = range(9)


WEIGHT_RELATIVE = True
GATHER_FINE = (0, 1)
SCATTER_FINE = (2, 3)

ORDER = (
    (6, 0, 0), (1, 0, 0), (0, 0, 0), (0, 1, 0), (1, 3, 0), (1, 1, 0), (1, 2, 0), (1, 0, 101),
    (0, 0, 110), (0, 0, 120), (1, 1, 101), (0, 1, 120), (1, 0, 102), (0, 0, 111), (0, 2, 0), (0,
    0, 101), (0, 0, 121), (0, 3, 0), (1, 1, 102), (1, 0, 111), (1, 0, 103), (1, 0, 110), (0, 1,
    110), (0, 1, 101), (0, 0, 122), (0, 0, 102), (0, 0, 112), (0, 2, 1), (1, 1, 111), (1, 0,
    104), (1, 1, 103), (0, 3, 1), (0, 1, 121), (1, 2, 1), (0, 0, 123), (0, 1, 111), (1, 0, 113),
    (1, 0, 112), (0, 0, 103), (1, 0, 114), (0, 0, 113), (1, 3, 1), (1, 2, 2), (1, 1, 113), (6,
    0, 1), (0, 3, 2), (1, 0, 6), (0, 1, 122), (0, 1, 112), (1, 1, 112), (0, 0, 6), (1, 1, 110),
    (0, 1, 102), (2, 0, 0), (0, 2, 2), (1, 3, 2), (1, 1, 104), (7, 0, 0), (1, 2, 3), (1, 1,
    114), (2, 0, 1), (0, 1, 103), (0, 1, 113), (7, 0, 1), (0, 1, 123), (1, 3, 3), (1, 1, 6), (0,
    3, 3), (6, 0, 2), (1, 2, 4), (2, 0, 2), (0, 1, 6), (0, 2, 3), (7, 1, 0), (7, 0, 2), (1, 3,
    4), (2, 0, 3), (0, 3, 4), (2, 1, 0), (0, 2, 4), (7, 1, 1), (7, 0, 3), (1, 2, 5), (0, 2, 5),
    (2, 1, 1), (1, 3, 5), (7, 1, 2), (8, 0, 4), (4, 0, 0), (1, 2, 6), (2, 1, 2), (0, 2, 6), (7,
    2, 0), (0, 3, 5), (1, 3, 6), (3, 0, 0), (7, 1, 3), (2, 2, 0), (2, 1, 3), (7, 2, 1), (3, 0,
    1), (0, 3, 6), (5, 0, 5), (4, 0, 1), (2, 3, 0), (2, 2, 1), (7, 3, 0), (8, 1, 4), (3, 1, 0),
    (5, 0, 1), (3, 0, 2), (7, 2, 2), (3, 1, 1), (4, 0, 2), (4, 1, 0), (2, 2, 2), (3, 0, 3), (7,
    3, 1), (5, 0, 2), (3, 1, 2), (7, 2, 3), (4, 1, 1), (5, 3, 1), (2, 2, 3), (2, 3, 1), (5, 3,
    0), (7, 3, 2), (4, 0, 3), (3, 1, 3), (5, 3, 3), (8, 2, 4), (4, 2, 0), (2, 3, 2), (3, 2, 0),
    (5, 0, 0), (4, 0, 4), (5, 1, 0), (4, 1, 2), (7, 3, 3), (4, 2, 114), (3, 0, 4), (3, 2, 121),
    (3, 2, 111), (4, 2, 113), (2, 3, 3), (3, 2, 101), (6, 0, 3), (5, 0, 3), (4, 1, 3), (4, 2,
    104), (5, 1, 4), (3, 2, 122), (4, 2, 112), (3, 0, 5), (5, 1, 3), (4, 0, 5), (3, 2, 112), (8,
    3, 4), (4, 1, 4), (4, 3, 0), (3, 3, 0), (4, 2, 103), (4, 0, 6), (3, 2, 113), (4, 3, 114),
    (4, 2, 111), (3, 3, 121), (3, 3, 111), (3, 1, 4), (5, 0, 4), (4, 3, 113), (3, 3, 101), (3,
    2, 102), (4, 3, 110), (4, 3, 104), (4, 2, 110), (3, 3, 122), (3, 2, 123), (5, 3, 4), (3, 3,
    112), (5, 1, 1), (4, 3, 112), (3, 3, 102), (4, 3, 103), (4, 2, 102), (3, 3, 123), (6, 0, 4),
    (3, 3, 113), (3, 1, 5), (4, 3, 111), (5, 2, 5), (5, 1, 2), (3, 2, 114), (4, 3, 102), (5, 2,
    1), (3, 2, 103), (3, 2, 124), (4, 1, 5), (5, 3, 5), (3, 3, 103), (3, 3, 114), (4, 2, 101),
    (3, 3, 124), (5, 2, 2), (3, 0, 6), (4, 3, 101), (5, 2, 0), (5, 2, 4), (5, 2, 3), (5, 3, 2),
    (3, 3, 104), (3, 1, 6), (5, 1, 5), (4, 2, 6), (3, 2, 104), (4, 1, 6), (3, 2, 6), (3, 3, 6),
    (4, 3, 6),
)


def scramble(hashed):
    hashed = hashed * jnp.int32(739982445)
    hashed = hashed ^ jnp.right_shift(hashed, 15) & jnp.int32(131071)
    hashed = hashed * jnp.int32(695872825)
    hashed = hashed ^ jnp.right_shift(hashed, 13) & jnp.int32(524287)
    return hashed


def kernel(
    cols_a, cut, early, seed_ref, grad_hbm, layer_hbm, gain_hbm, pre_hbm, w1_hbm, w2_hbm,
    final, grad_out, layer_out, gain_out, wg_hbm,
    grad_ref, branch, G, H, W1, W2, PH, RY1A, RY2A, RY1B, RY2B, ACT, N, RA4, RA, RAX2, RAX1, RB2, RB1, RBZ4, RBZ,
    WACC, WGR, ssem, rsem, lsem,
):
    s = lax.axis_index("section")
    t = lax.axis_index("tensor")
    q = lax.axis_index("dp")
    x, z = t // Z, t % Z
    rows = grad_ref.shape[0]
    width = grad_ref.shape[1]
    block = width // Y
    hidden_cols = H.shape[-1]
    tok = H.shape[1]
    shard = tok // Y
    half = shard // 2
    A, B = pl.ds(0, cols_a), pl.ds(cols_a, block - cols_a)

    def xi(d):
        return (x + d + X) % X

    def zi(d):
        return (z + d + Z) % Z

    def yi(d):
        return (q + d + Y) % Y

    to = {
        "x+": (s, xi(1) * Z + z, q),
        "x-": (s, xi(-1) * Z + z, q),
        "z+": (s, x * Z + zi(1), q),
        "z-": (s, x * Z + zi(-1), q),
        "y+": (s, t, yi(1)),
        "y-": (s, t, yi(-1)),
        "y2": (s, t, yi(2)),
        "x2": (s, xi(2) * Z + z, q),
        "c": (1 - s, t, q),
        "cy+": (1 - s, t, yi(1)),
        "cy-": (1 - s, t, yi(-1)),
        "cy2": (1 - s, t, yi(2)),
    }
    tile = 256
    count = [0]
    pending = {}

    def send(*parts, whole=None):
        i = count[0]
        count[0] += 1
        slot = i % SLOTS
        if slot in pending:
            pending.pop(slot).wait_send()

        def copy(src, dst, where):
            return pltpu.make_async_remote_copy(
                src_ref=src, dst_ref=dst, send_sem=ssem.at[slot], recv_sem=rsem.at[i],
                device_id=to[where], device_id_type=MESH,
            )

        for part in parts:
            started = copy(*part)
            started.start()
        pending[slot] = started if whole is None else copy(whole, whole, parts[0][2])
        return (pending[slot],)

    def drain():
        for c in pending.values():
            c.wait_send()
        pending.clear()

    with jax.named_scope("start"):
        barrier = pltpu.get_barrier_semaphore()
        for where in to.values():
            pl.semaphore_signal(barrier, inc=1, device_id=where, device_id_type=MESH)
        load_grad = pltpu.make_async_copy(grad_hbm, grad_ref, lsem.at[9])
        load_grad.start()
        load_pre = pltpu.make_async_copy(pre_hbm, H.at[q], lsem.at[0])
        load_w2 = pltpu.make_async_copy(w2_hbm, W2, lsem.at[1])
        load_w1 = pltpu.make_async_copy(w1_hbm, W1, lsem.at[2])
        load_pre.start()
        load_w2.start()
        load_w1.start()
        load_grad.wait()

        offset = (seed_ref[0] * jnp.int32(131) + q) * jnp.int32(1640531527)
        row_ids = t * rows + lax.broadcasted_iota(jnp.int32, (rows, block), 0)
        col_ids = lax.broadcasted_iota(jnp.int32, (rows, block), 1)
        base = row_ids * jnp.int32(width) + col_ids + offset
        for j in range(Y):
            hashed = scramble(base + jnp.int32(j * block))
            kept = (jnp.right_shift(hashed, 9) & jnp.int32(1023)) < jnp.int32(922)
            factor = jnp.where(kept, F32(KEEP_SCALE), F32(0.0))
            branch[j] = (grad_ref[:, j * block:(j + 1) * block].astype(F32) * factor).astype(BF)
        G[q, x, z] = branch[q]
        load_pre.wait()
        H[q] = jnp.maximum(H[q], jnp.zeros((), BF))

    with jax.named_scope("barrier"):
        pl.semaphore_wait(barrier, len(to))

    first = []
    for d, where in ((1, "y+"), (3, "y-"), (2, "y2")):
        first += send((branch.at[yi(d)], G.at[q, x, z], where))
    shared = []
    for src, dst in ((grad_hbm, grad_out), (layer_hbm, layer_out), (gain_hbm, gain_out)):
        shared += send((src, dst, "c"))

    st = {}

    def hidden_step(k):
        def piece(mb, part, rows_from, rows_count):
            return H.at[mb, pl.ds(pl.multiple_of(part * shard + rows_from, half), rows_count)]

        if k == 0:
            st["h1"] = same(H.at[q], "y+", H.at[q], "y-", whole=H.at[pl.ds(0, 2)])
        elif k == 1:
            wait2("h1")
            st["h2"] = same(
                piece(yi(-1), yi(1), 0, half), "y+", piece(yi(1), yi(-1), half, half), "y-",
                whole=H.at[0, pl.ds(0, shard)],
            )
        elif k == 2:
            wait2("h2")
        elif k == 3:
            st["h3"] = same(
                piece(yi(-1), yi(2), 0, shard), "y+", piece(yi(1), yi(2), 0, shard), "y-",
                whole=H.at[0, pl.ds(0, 2 * shard)],
            ) + same(
                piece(yi(-1), yi(3), 0, half), "y+", piece(yi(1), yi(1), half, half), "y-",
                whole=H.at[0, pl.ds(0, shard)],
            )
        else:
            wait2("h3")

    def wait2(key):
        for c in st.pop(key):
            c.wait_recv()

    def same(ref, where, other=None, other_where=None, whole=None):
        if other is None:
            return send((ref, ref, where))
        return send((ref, ref, where), (other, other, other_where), whole=whole)


    groups = ((0,), (1, -1), (2,))
    slot_of = {0: 0, 1: 1, -1: 2, 2: 3}

    def many(parts, two, four):
        return send(*parts, whole=(None, two, None, four)[len(parts) - 1])

    def gather_a(m, k):
        two, four = RAX1.at[m], RA4.at[m]

        def on(g, d):
            parts = []
            for dx in groups[g]:
                up, down = G.at[m, xi(dx), zi(-d), :, A], G.at[m, xi(dx), zi(d), :, A]
                if d < 3 or dx in (0, 1):
                    parts.append((up, up, "z+"))
                if d < 3 or dx in (-1, 2):
                    parts.append((down, down, "z-"))
            st["ga", m, g] = many(parts, two, four)

        if k == 0:
            own = G.at[m, x, z, :, A]
            st["gx1", m] = same(own, "x+", own, "x-", whole=two)
            on(0, 0)
            st["gx2", m] = same(own, "x2")
        elif k == 6:
            for g in range(3):
                wait2(("ga", m, g))
        elif k in (110, 120):
            wait2(("gx1" if k == 110 else "gx2", m))
            on((k - 100) // 10, 0)
        else:
            g = (k - 100) // 10
            wait2(("ga", m, g))
            on(g, k % 10)

    def gather_b(m, k):
        two, four = RBZ.at[m, :, 0], RB2.at[m, 0]

        def piece(dx, dz):
            return G.at[m, xi(dx), zi(dz), :, B]

        def along_z(d):
            parts = [(piece(0, -d), piece(0, -d), "z+")]
            if d < 3:
                parts.append((piece(0, d), piece(0, d), "z-"))
            st["gz", m, d] = many(parts, two, four)

        def along_x(d):
            parts = []
            for dz in ((d,) if d in (0, 4) else (d, -d)):
                parts += [(piece(0, dz), piece(0, dz), w) for w in ("x+", "x-")]
            st["gx", m, d] = many(parts, two, four)

        if k == 0:
            along_z(0)
            along_x(0)
        elif k == 6:
            for d in range(5):
                wait2(("gf", m, d))
        elif k < 105:
            d = k - 100
            wait2(("gz", m, d - 1))
            if d < 4:
                along_z(d)
            along_x(d)
        else:
            d = k - 110
            wait2(("gx", m, d))
            parts = []
            if d < 4:
                parts.append((piece(-1, d), piece(-1, d), "x+"))
            if d > 0:
                parts.append((piece(1, -d), piece(1, -d), "x-"))
            st["gf", m, d] = many(parts, two, four)

    def scatter_a(m, k):
        two, four = RAX1.at[m], RA4.at[m]
        every = slice(None)

        def on(g, step):
            parts, d = [], 4 - step
            for dx in groups[g]:
                i = slot_of[dx]
                if step == 0:
                    parts.append(
                        (N.at[m, xi(dx), zi(4), :, A], RA4.at[m, i // 2, i % 2],
                         "z+" if dx in (0, 1) else "z-")
                    )
                else:
                    parts += [
                        (N.at[m, xi(dx), zi(d), :, A], RA.at[m, 0, d - 1, i], "z+"),
                        (N.at[m, xi(dx), zi(-d), :, A], RA.at[m, 1, d - 1, i], "z-"),
                    ]
            st["sa", m, g] = many(parts, two, four)

        if k == 0:
            norm_part(m, pl.ds(0, early))
            for g in (2, 1, 0):
                on(g, 0)
        elif k == 6:
            wait2(("sx", m, 1))
            wait2(("sx", m, 2))
            index = (m, x, z, every, A)
            total = N[index].astype(F32) + RAX1[m, 0].astype(F32) + RAX1[m, 1].astype(F32)
            N[index] = (total + RAX2[m].astype(F32)).astype(BF)
        else:
            g, step = (k - 100) // 10, k % 10
            d = 4 - step
            wait2(("sa", m, g))
            for dx in groups[g]:
                i = slot_of[dx]
                if step == 1:
                    there = zi(3) if dx in (0, 1) else zi(-3)
                    add((m, xi(dx), there, every, A), RA4[m, i // 2, i % 2])
                elif step < 4:
                    add((m, xi(dx), zi(d), every, A), RA[m, 0, d, i])
                    add((m, xi(dx), zi(-d), every, A), RA[m, 1, d, i])
                else:
                    index = (m, xi(dx), z, every, A)
                    N[index] = (
                        N[index].astype(F32) + RA[m, 0, 0, i].astype(F32) + RA[m, 1, 0, i].astype(F32)
                    ).astype(BF)
            if step < 4:
                on(g, step)
            elif g == 1:
                st["sx", m, 1] = send(
                    (N.at[m, xi(1), z, :, A], RAX1.at[m, 0], "x+"),
                    (N.at[m, xi(-1), z, :, A], RAX1.at[m, 1], "x-"),
                    whole=two,
                )
            elif g == 2:
                st["sx", m, 2] = send((N.at[m, xi(2), z, :, A], RAX2.at[m], "x2"))

    def scatter_b(m, k):
        two, four = RBZ.at[m, :, 0], RB2.at[m, 0]
        every = slice(None)

        def both(d):
            return ((d, d),) if d in (0, 4) else ((d, d), (-d, Z - d))

        def summed(dz, refs):
            index = (m, x, zi(dz), every, B)
            total = N[index].astype(F32)
            for ref in refs:
                total += ref[...].astype(F32)
            N[index] = total.astype(BF)

        if k == 0:
            for d in (4, 3, 2, 1, 0):
                parts = []
                if d < 4:
                    parts.append((N.at[m, xi(2), zi(d), :, B], RB2.at[m, 0, d], "x+"))
                if d > 0:
                    parts.append((N.at[m, xi(2), zi(-d), :, B], RB2.at[m, 1, d - 1], "x-"))
                st["sf", m, d] = many(parts, two, four)
        elif k >= 110:
            d = k - 110
            wait2(("sf", m, d))
            if d < 4:
                add((m, xi(1), zi(d), every, B), RB2[m, 0, d])
            if d > 0:
                add((m, xi(-1), zi(-d), every, B), RB2[m, 1, d - 1])
            parts = []
            for dz, i in both(d):
                parts += [
                    (N.at[m, xi(1), zi(dz), :, B], RB1.at[m, 0, i], "x+"),
                    (N.at[m, xi(-1), zi(dz), :, B], RB1.at[m, 1, i], "x-"),
                ]
            st["sn", m, d] = many(parts, two, four)
        else:
            d = k - 100 if k > 6 else 0
            wait2(("sn", m, d))
            if d < 4:
                wait2(("sz", m, d + 1))
            for dz, i in both(d):
                refs = [RB1.at[m, 0, i], RB1.at[m, 1, i]]
                if d == 3 and dz == 3:
                    refs.append(RBZ4.at[m])
                elif d == 0:
                    refs += [RBZ.at[m, 0, 0], RBZ.at[m, 1, 0]]
                elif d < 3:
                    refs.append(RBZ.at[m, 0 if dz > 0 else 1, d])
                summed(dz, refs)
            if d == 4:
                st["sz", m, 4] = send((N.at[m, x, zi(4), :, B], RBZ4.at[m], "z+"))
            elif d > 0:
                st["sz", m, d] = send(
                    (N.at[m, x, zi(d), :, B], RBZ.at[m, 0, d - 1], "z+"),
                    (N.at[m, x, zi(-d), :, B], RBZ.at[m, 1, d - 1], "z-"),
                    whole=RBZ.at[m, :, d - 1],
                )

    def ag_a(m, k):
        if m in GATHER_FINE:
            return gather_a(m, k)
        key = ("aga", m)
        if k > 0:
            wait2(key)
        if k == 0:
            own = G.at[m, x, z, :, A]
            st[key] = same(own, "x+", own, "x-", whole=RAX1.at[m])
        elif k == 1:
            if m % 2 == 0:
                st[key] = same(G.at[m, xi(-1), z, :, A], "x+")
            else:
                st[key] = same(G.at[m, xi(1), z, :, A], "x-")
        elif k < 5:
            d = k - 2
            st[key] = same(
                G.at[m, :, zi(-d), :, A], "z+", G.at[m, :, zi(d), :, A], "z-", whole=RA.at[m, :, 0]
            )
        elif k == 5:
            st[key] = same(
                G.at[m, pl.ds(0, 2), zi(-3), :, A], "z+", G.at[m, pl.ds(2, 2), zi(3), :, A], "z-",
                whole=RA4.at[m],
            )

    def ag_b(m, k):
        if m in GATHER_FINE:
            return gather_b(m, k)
        key = ("agb", m)
        if k > 0:
            wait2(key)
        if k < 3:
            st[key] = same(
                G.at[m, x, zi(-k), :, B], "z+", G.at[m, x, zi(k), :, B], "z-", whole=RBZ.at[m, :, 0]
            )
        elif k == 3:
            if m % 2 == 0:
                st[key] = same(G.at[m, x, zi(-3), :, B], "z+")
            else:
                st[key] = same(G.at[m, x, zi(3), :, B], "z-")
        elif k == 4:
            own = G.at[m, x, :, :, B]
            st[key] = same(own, "x+", own, "x-", whole=RB1.at[m])
        elif k == 5:
            st[key] = same(
                G.at[m, xi(-1), pl.ds(0, 4), :, B], "x+", G.at[m, xi(1), pl.ds(4, 4), :, B], "x-",
                whole=RB2.at[m],
            )

    parts = ((0, cut, RY1A, RY2A), (cut, hidden_cols - cut, RY1B, RY2B))

    def y_step(j, m, k):
        key = ("y", j, m)
        start, size, R1, R2 = parts[j]
        cols = pl.ds(start, size)
        lo, hi = pl.ds(0, half), pl.ds(half, half)
        if k > 0:
            wait2(key)
        if k == 0:
            if m == 0 and j == 0:
                load_w2.wait()
            part = jnp.dot(G[m].reshape(tok, block), W2[:, cols], preferred_element_type=F32)
            PH[m, :, :, cols] = part.astype(BF).reshape(Y, shard, size)
            st[key] = send(
                (PH.at[m, yi(2), lo, cols], R1.at[m, 0], "y+"),
                (PH.at[m, yi(2), hi, cols], R1.at[m, 1], "y-"),
                whole=R1.at[m],
            )
        elif k == 1:
            PH[m, yi(1), lo, cols] = PH[m, yi(1), lo, cols] + R1[m, 0]
            PH[m, yi(-1), hi, cols] = PH[m, yi(-1), hi, cols] + R1[m, 1]
            st[key] = send(
                (PH.at[m, yi(1), :, cols], R2.at[m, 0], "y+"),
                (PH.at[m, yi(-1), :, cols], R2.at[m, 1], "y-"),
                whole=R2.at[m],
            )
        elif k == 2:
            total = PH[m, q, :, cols].astype(F32) + R2[m, 0].astype(F32) + R2[m, 1].astype(F32)
            mine = pl.ds(pl.multiple_of(q * shard, shard), shard)
            ACT[m, q, :, cols] = jnp.where(
                H[m, mine, cols].astype(F32) > 0, total, F32(0.0)
            ).astype(BF)
            own = ACT.at[m, q, :, cols]
            st[key] = same(own, "y+", own, "y-", whole=R2.at[m])
        elif k == 3:
            st[key] = same(
                ACT.at[m, yi(-1), lo, cols], "y+", ACT.at[m, yi(1), hi, cols], "y-", whole=R1.at[m]
            )

    def norm_part(m, cols):
        part = jnp.dot(ACT[m].reshape(tok, hidden_cols), W1[:, cols], preferred_element_type=F32)
        N[m, :, :, :, cols] = part.astype(BF).reshape(X, Z, rows, cols.size)

    def mm_step(m, k):
        if m == 0:
            load_w1.wait()
        wait2(("y", 0, m))
        wait2(("y", 1, m))
        norm_part(m, pl.ds(early, block - early))

    def add(index, received):
        N[index] = N[index] + received

    def rs_a(m, k):
        if m in SCATTER_FINE:
            return scatter_a(m, k)
        key = ("rsa", m)
        if k > 0:
            wait2(key)
        lo, hi = pl.ds(0, 2), pl.ds(2, 2)
        if k == 0:
            norm_part(m, pl.ds(0, early))
            st[key] = send(
                (N.at[m, lo, zi(4), :, A], RA4.at[m, 0], "z+"),
                (N.at[m, hi, zi(4), :, A], RA4.at[m, 1], "z-"),
                whole=RA4.at[m],
            )
        elif k < 4:
            d = 4 - k
            if k == 1:
                add((m, lo, zi(3), slice(None), A), RA4[m, 0])
                add((m, hi, zi(-3), slice(None), A), RA4[m, 1])
            else:
                add((m, slice(None), zi(d), slice(None), A), RA[m, 0, d])
                add((m, slice(None), zi(-d), slice(None), A), RA[m, 1, d])
            st[key] = send(
                (N.at[m, :, zi(d), :, A], RA.at[m, 0, d - 1], "z+"),
                (N.at[m, :, zi(-d), :, A], RA.at[m, 1, d - 1], "z-"),
                whole=RA.at[m, :, d - 1],
            )
        elif k == 4:
            index = (m, slice(None), z, slice(None), A)
            N[index] = (
                N[index].astype(F32) + RA[m, 0, 0].astype(F32) + RA[m, 1, 0].astype(F32)
            ).astype(BF)
            st[key] = send((N.at[m, xi(2), z, :, A], RAX2.at[m], "x+" if m % 2 == 0 else "x-"))
        elif k == 5:
            far = xi(1) if m % 2 == 0 else xi(-1)
            add((m, far, z, slice(None), A), RAX2[m])
            st[key] = send(
                (N.at[m, xi(1), z, :, A], RAX1.at[m, 0], "x+"),
                (N.at[m, xi(-1), z, :, A], RAX1.at[m, 1], "x-"),
                whole=RAX1.at[m],
            )
        else:
            index = (m, x, z, slice(None), A)
            N[index] = (
                N[index].astype(F32) + RAX1[m, 0].astype(F32) + RAX1[m, 1].astype(F32)
            ).astype(BF)

    def rs_b(m, k):
        if m in SCATTER_FINE:
            return scatter_b(m, k)
        key = ("rsb", m)
        if k > 0:
            wait2(key)
        lo, hi = pl.ds(0, 4), pl.ds(4, 4)
        every = slice(None)
        if k == 0:
            st[key] = send(
                (N.at[m, xi(2), lo, :, B], RB2.at[m, 0], "x+"),
                (N.at[m, xi(2), hi, :, B], RB2.at[m, 1], "x-"),
                whole=RB2.at[m],
            )
        elif k == 1:
            add((m, xi(1), lo, every, B), RB2[m, 0])
            add((m, xi(-1), hi, every, B), RB2[m, 1])
            st[key] = send(
                (N.at[m, xi(1), :, :, B], RB1.at[m, 0], "x+"),
                (N.at[m, xi(-1), :, :, B], RB1.at[m, 1], "x-"),
                whole=RB1.at[m],
            )
        elif k == 2:
            index = (m, x, every, every, B)
            N[index] = (
                N[index].astype(F32) + RB1[m, 0].astype(F32) + RB1[m, 1].astype(F32)
            ).astype(BF)
            st[key] = send((N.at[m, x, zi(4), :, B], RBZ4.at[m], "z+" if m % 2 == 0 else "z-"))
        elif k < 6:
            d = 6 - k
            if k == 3:
                add((m, x, zi(3) if m % 2 == 0 else zi(-3), every, B), RBZ4[m])
            else:
                add((m, x, zi(d), every, B), RBZ[m, 0, d])
                add((m, x, zi(-d), every, B), RBZ[m, 1, d])
            st[key] = send(
                (N.at[m, x, zi(d), :, B], RBZ.at[m, 0, d - 1], "z+"),
                (N.at[m, x, zi(-d), :, B], RBZ.at[m, 1, d - 1], "z-"),
                whole=RBZ.at[m, :, d - 1],
            )
        else:
            index = (m, x, z, every, B)
            N[index] = (
                N[index].astype(F32) + RBZ[m, 0, 0].astype(F32) + RBZ[m, 1, 0].astype(F32)
            ).astype(BF)

    taken = [0] * (block // tile)

    def weight_grad(m, j):
        cols = pl.ds(j * tile, tile)
        mb = yi(m) if WEIGHT_RELATIVE else m
        part = lax.dot_general(
            G[mb, :, :, :, cols].reshape(tok, tile), H[mb], (((0,), (0,)), ((), ())),
            preferred_element_type=F32,
        )
        taken[j] += 1
        if taken[j] == 1:
            WACC[cols] = part
        elif taken[j] < Y:
            WACC[cols] += part
        else:
            WGR[cols] = (WACC[cols] + part).astype(BF)
            c = pltpu.make_async_copy(WGR.at[cols], wg_hbm.at[cols], lsem.at[3 + j])
            c.start()
            outs.append(c)

    outs = []

    with jax.named_scope("first"):
        for c in first:
            c.wait_recv()

    steps = {
        AG_A: ag_a, AG_B: ag_b, RS_A: rs_a, RS_B: rs_b, MM: mm_step,
        Y_LO: functools.partial(y_step, 0), Y_HI: functools.partial(y_step, 1),
    }
    for kind, m, k in ORDER:
        if kind == WG:
            weight_grad(m, k)
        elif kind == HF:
            hidden_step(k)
        else:
            steps[kind](m, k)

    with jax.named_scope("last"):
        last = []
        for d, where in ((1, "cy+"), (3, "cy-"), (2, "cy2"), (0, "c")):
            last += send((N.at[yi(d), x, z], final.at[q], where))
        drain()
        for c in outs:
            c.wait()
        for c in shared:
            c.wait_recv()
        for c in last:
            c.wait_recv()


STRIPS = 8


def norm_back(final, grad, layer, gain, wg_in, out, wg_out, fin, up, lay, gai, res, wg, sems):
    strips = [pl.ds(i * (wg.shape[0] // STRIPS), wg.shape[0] // STRIPS) for i in range(STRIPS)]
    ins = [pltpu.make_async_copy(wg_in.at[r], wg.at[r], sems.at[6 + i]) for i, r in enumerate(strips)]
    outs = [pltpu.make_async_copy(wg.at[r], wg_out.at[r], sems.at[6 + i]) for i, r in enumerate(strips)]
    loads = [
        pltpu.make_async_copy(src, dst, sems.at[1 + i])
        for i, (src, dst) in enumerate(((layer, lay), (final, fin), (gain, gai), (grad, up)))
    ]
    for c in loads:
        c.start()
    for c in ins:
        c.start()
    width = lay.shape[1]
    block = width // Y
    loads[0].wait()
    values = lay[...].astype(F32)
    center = values - jnp.mean(values, axis=-1, keepdims=True)
    scale = lax.rsqrt(jnp.mean(center * center, axis=-1, keepdims=True) + NORM_EPS)
    for c in loads[1:]:
        c.wait()
    for i in range(STRIPS):
        ins[i].wait()
        outs[i].start()
    total = jnp.zeros((lay.shape[0], 1), F32)
    dotted = jnp.zeros((lay.shape[0], 1), F32)
    for j in range(Y):
        cols = slice(j * block, (j + 1) * block)
        scaled = fin[j].astype(F32) * gai[:, cols]
        total += jnp.sum(scaled, axis=-1, keepdims=True)
        dotted += jnp.sum(scaled * (center[:, cols] * scale), axis=-1, keepdims=True)
    total = total / width
    dotted = dotted / width
    for j in range(Y):
        cols = slice(j * block, (j + 1) * block)
        scaled = fin[j].astype(F32) * gai[:, cols]
        bracket = scaled - total - (center[:, cols] * scale) * dotted
        res[:, cols] = (up[:, cols].astype(F32) + scale * bracket).astype(BF)
    store = pltpu.make_async_copy(res, out, sems.at[5])
    store.start()
    store.wait()
    for c in outs:
        c.wait()


SPLIT = 640
SLOTS = 48
COPIES = 3 + 3 + 4 + Y * 32 + 4 + 16 * (len(GATHER_FINE) + len(SCATTER_FINE))


def shards(grad_out, drop_seed, layer_in, ln_gain, pre_act, fc1_weight, fc2_weight):
    rows, width = grad_out.shape[2:]
    tok, hidden = pre_act.shape[2:]
    block = width // Y
    a = SPLIT
    b = block - a
    shard = tok // Y
    cut = hidden // 3
    early = block // 3
    anyspace = pl.BlockSpec(memory_space=pl.ANY)
    final, grad_there, layer_there, gain_there, weight_grad = pl.pallas_call(
        functools.partial(kernel, a, cut, early),
        out_shape=(
            jax.ShapeDtypeStruct((Y, rows, block), BF),
            jax.ShapeDtypeStruct((rows, width), BF),
            jax.ShapeDtypeStruct((rows, width), BF),
            jax.ShapeDtypeStruct((1, width), F32),
            jax.ShapeDtypeStruct((block, hidden), BF),
        ),
        in_specs=[pl.BlockSpec(memory_space=pltpu.SMEM)] + [anyspace] * 6,
        out_specs=(anyspace,) * 5,
        scratch_shapes=[
            pltpu.VMEM((rows, width), BF),
            pltpu.VMEM((Y, rows, block), BF),
            pltpu.VMEM((Y, X, Z, rows, block), BF),
            pltpu.VMEM((Y, tok, hidden), BF),
            pltpu.VMEM((hidden, block), BF),
            pltpu.VMEM((block, hidden), BF),
            pltpu.VMEM((Y, Y, shard, hidden), BF),
            pltpu.VMEM((Y, 2, shard // 2, cut), BF),
            pltpu.VMEM((Y, 2, shard, cut), BF),
            pltpu.VMEM((Y, 2, shard // 2, hidden - cut), BF),
            pltpu.VMEM((Y, 2, shard, hidden - cut), BF),
            pltpu.VMEM((Y, Y, shard, hidden), BF),
            pltpu.VMEM((Y, X, Z, rows, block), BF),
            pltpu.VMEM((Y, 2, X // 2, rows, a), BF),
            pltpu.VMEM((Y, 2, 3, X, rows, a), BF),
            pltpu.VMEM((Y, rows, a), BF),
            pltpu.VMEM((Y, 2, rows, a), BF),
            pltpu.VMEM((Y, 2, Z // 2, rows, b), BF),
            pltpu.VMEM((Y, 2, Z, rows, b), BF),
            pltpu.VMEM((Y, rows, b), BF),
            pltpu.VMEM((Y, 2, 3, rows, b), BF),
            pltpu.VMEM((block, hidden), F32),
            pltpu.VMEM((block, hidden), BF),
            pltpu.SemaphoreType.DMA((SLOTS,)),
            pltpu.SemaphoreType.DMA((COPIES,)),
            pltpu.SemaphoreType.DMA((10,)),
        ],
        compiler_params=pltpu.CompilerParams(
            collective_id=0, has_side_effects=True, vmem_limit_bytes=60 * 1024 * 1024
        ),
    )(
        drop_seed, grad_out[0, 0], layer_in[0, 0], ln_gain,
        pre_act[0, 0], fc1_weight[0], fc2_weight[0],
    )
    arriving, weight_grad = pl.pallas_call(
        norm_back,
        out_shape=(
            jax.ShapeDtypeStruct((rows, width), BF),
            jax.ShapeDtypeStruct((block, hidden), BF),
        ),
        in_specs=[anyspace] * 5,
        out_specs=(anyspace,) * 2,
        scratch_shapes=[
            pltpu.VMEM((Y, rows, block), BF),
            pltpu.VMEM((rows, width), BF),
            pltpu.VMEM((rows, width), BF),
            pltpu.VMEM((1, width), F32),
            pltpu.VMEM((rows, width), BF),
            pltpu.VMEM((block, hidden), BF),
            pltpu.SemaphoreType.DMA((6 + STRIPS,)),
        ],
    )(final, grad_there, layer_there, gain_there, weight_grad)
    return (arriving[None, None], weight_grad[None])


def solution(mesh):
    placed = (
        P("section", "dp", "tensor", None),
        P("section"),
        P("section", "dp", "tensor", None),
        P("section", None),
        P("section", "dp", None, "tensor"),
        P("section", "tensor", "dp"),
        P("section", "dp", "tensor"),
    )
    return jax.shard_map(
        shards,
        mesh=mesh,
        in_specs=placed,
        out_specs=(P("section", "dp", "tensor", None), P("section", "dp", "tensor")),
        check_vma=False,
    )
```

```python
import functools

import jax
import jax.numpy as jnp
from jax import lax
from jax.experimental import pallas as pl
from jax.experimental.pallas import tpu as pltpu
from jax.sharding import PartitionSpec as P

KEEP_SCALE = 1.0 / 0.9
NORM_EPS = 1e-05
MESH = pl.DeviceIdType.MESH
X, Z, Y = 4, 8, 4
BF, F32 = jnp.bfloat16, jnp.float32

AG_A, AG_B, Y_LO, RS_A, RS_B, WG, HF, Y_HI, MM = range(9)


WEIGHT_RELATIVE = True
GATHER_FINE = (0, 1)
SCATTER_FINE = (2, 3)

ORDER = (
    (6, 0, 0), (1, 0, 0), (0, 0, 0), (0, 1, 0), (1, 3, 0), (1, 1, 0), (1, 2, 0), (1, 0, 101),
    (0, 0, 110), (0, 0, 120), (1, 1, 101), (0, 1, 120), (1, 0, 102), (0, 0, 111), (0, 2, 0), (0,
    0, 101), (0, 0, 121), (0, 3, 0), (1, 1, 102), (1, 0, 111), (1, 0, 103), (1, 0, 110), (0, 1,
    110), (0, 1, 101), (0, 0, 122), (0, 0, 102), (0, 0, 112), (0, 2, 1), (1, 1, 111), (1, 0,
    104), (1, 1, 103), (0, 3, 1), (0, 1, 121), (1, 2, 1), (0, 0, 123), (0, 1, 111), (1, 0, 113),
    (1, 0, 112), (0, 0, 103), (1, 0, 114), (0, 0, 113), (1, 3, 1), (1, 2, 2), (1, 1, 113), (6,
    0, 1), (0, 3, 2), (1, 0, 6), (0, 1, 122), (0, 1, 112), (1, 1, 112), (0, 0, 6), (1, 1, 110),
    (0, 1, 102), (2, 0, 0), (0, 2, 2), (1, 3, 2), (1, 1, 104), (7, 0, 0), (1, 2, 3), (1, 1,
    114), (2, 0, 1), (0, 1, 103), (0, 1, 113), (7, 0, 1), (0, 1, 123), (1, 3, 3), (1, 1, 6), (0,
    3, 3), (6, 0, 2), (1, 2, 4), (2, 0, 2), (0, 1, 6), (0, 2, 3), (7, 1, 0), (7, 0, 2), (1, 3,
    4), (2, 0, 3), (0, 3, 4), (2, 1, 0), (0, 2, 4), (7, 1, 1), (7, 0, 3), (1, 2, 5), (0, 2, 5),
    (2, 1, 1), (1, 3, 5), (7, 1, 2), (8, 0, 4), (4, 0, 0), (1, 2, 6), (2, 1, 2), (0, 2, 6), (7,
    2, 0), (0, 3, 5), (1, 3, 6), (3, 0, 0), (7, 1, 3), (2, 2, 0), (2, 1, 3), (7, 2, 1), (3, 0,
    1), (0, 3, 6), (5, 0, 5), (4, 0, 1), (2, 3, 0), (2, 2, 1), (7, 3, 0), (8, 1, 4), (3, 1, 0),
    (5, 0, 1), (3, 0, 2), (7, 2, 2), (3, 1, 1), (4, 0, 2), (4, 1, 0), (2, 2, 2), (3, 0, 3), (7,
    3, 1), (5, 0, 2), (3, 1, 2), (7, 2, 3), (4, 1, 1), (5, 3, 1), (2, 2, 3), (2, 3, 1), (5, 3,
    0), (7, 3, 2), (4, 0, 3), (3, 1, 3), (5, 3, 3), (8, 2, 4), (4, 2, 0), (2, 3, 2), (3, 2, 0),
    (5, 0, 0), (4, 0, 4), (5, 1, 0), (4, 1, 2), (7, 3, 3), (4, 2, 114), (3, 0, 4), (3, 2, 121),
    (3, 2, 111), (4, 2, 113), (2, 3, 3), (3, 2, 101), (6, 0, 3), (5, 0, 3), (4, 1, 3), (4, 2,
    104), (5, 1, 4), (3, 2, 122), (4, 2, 112), (3, 0, 5), (5, 1, 3), (4, 0, 5), (3, 2, 112), (8,
    3, 4), (4, 1, 4), (4, 3, 0), (3, 3, 0), (4, 2, 103), (4, 0, 6), (3, 2, 113), (4, 3, 114),
    (4, 2, 111), (3, 3, 121), (3, 3, 111), (3, 1, 4), (5, 0, 4), (4, 3, 113), (3, 3, 101), (3,
    2, 102), (4, 3, 110), (4, 3, 104), (4, 2, 110), (3, 3, 122), (3, 2, 123), (5, 3, 4), (3, 3,
    112), (5, 1, 1), (4, 3, 112), (3, 3, 102), (4, 3, 103), (4, 2, 102), (3, 3, 123), (6, 0, 4),
    (3, 3, 113), (3, 1, 5), (4, 3, 111), (5, 2, 5), (5, 1, 2), (3, 2, 114), (4, 3, 102), (5, 2,
    1), (3, 2, 103), (3, 2, 124), (4, 1, 5), (5, 3, 5), (3, 3, 103), (3, 3, 114), (4, 2, 101),
    (3, 3, 124), (5, 2, 2), (3, 0, 6), (4, 3, 101), (5, 2, 0), (5, 2, 4), (5, 2, 3), (5, 3, 2),
    (3, 3, 104), (3, 1, 6), (5, 1, 5), (4, 2, 6), (3, 2, 104), (4, 1, 6), (3, 2, 6), (3, 3, 6),
    (4, 3, 6),
)


def scramble(hashed):
    hashed = hashed * jnp.int32(739982445)
    hashed = hashed ^ jnp.right_shift(hashed, 15) & jnp.int32(131071)
    hashed = hashed * jnp.int32(695872825)
    hashed = hashed ^ jnp.right_shift(hashed, 13) & jnp.int32(524287)
    return hashed


def kernel(
    cols_a, cut, early, seed_ref, grad_hbm, layer_hbm, gain_hbm, pre_hbm, w1_hbm, w2_hbm,
    final, grad_out, layer_out, gain_out, wg_hbm,
    grad_ref, branch, G, H, W1, W2, PH, RY1A, RY2A, RY1B, RY2B, ACT, N, RA4, RA, RAX2, RAX1, RB2, RB1, RBZ4, RBZ,
    WACC, WGR, ssem, rsem, lsem, pace_sem,
):
    s = lax.axis_index("section")
    t = lax.axis_index("tensor")
    q = lax.axis_index("dp")
    x, z = t // Z, t % Z
    rows = grad_ref.shape[0]
    width = grad_ref.shape[1]
    block = width // Y
    hidden_cols = H.shape[-1]
    tok = H.shape[1]
    shard = tok // Y
    half = shard // 2
    A, B = pl.ds(0, cols_a), pl.ds(cols_a, block - cols_a)

    def xi(d):
        return (x + d + X) % X

    def zi(d):
        return (z + d + Z) % Z

    def yi(d):
        return (q + d + Y) % Y

    to = {
        "x+": (s, xi(1) * Z + z, q),
        "x-": (s, xi(-1) * Z + z, q),
        "z+": (s, x * Z + zi(1), q),
        "z-": (s, x * Z + zi(-1), q),
        "y+": (s, t, yi(1)),
        "y-": (s, t, yi(-1)),
        "y2": (s, t, yi(2)),
        "x2": (s, xi(2) * Z + z, q),
        "c": (1 - s, t, q),
        "cy+": (1 - s, t, yi(1)),
        "cy-": (1 - s, t, yi(-1)),
        "cy2": (1 - s, t, yi(2)),
    }
    tile = 256
    count = [0]
    pending = {}

    def send(*parts, whole=None, arrival=None):
        i = count[0]
        count[0] += 1
        slot = i % SLOTS
        landed = i if arrival is None else arrival
        if slot in pending:
            pending.pop(slot).wait_send()

        def copy(src, dst, where):
            return pltpu.make_async_remote_copy(
                src_ref=src, dst_ref=dst, send_sem=ssem.at[slot], recv_sem=rsem.at[landed],
                device_id=to[where] if isinstance(where, str) else where, device_id_type=MESH,
            )

        for part in parts:
            started = copy(*part)
            started.start()
        pending[slot] = started if whole is None else copy(whole, whole, parts[0][2])
        return (pending[slot],)

    def drain():
        for c in pending.values():
            c.wait_send()
        pending.clear()

    with jax.named_scope("start"):
        barrier = pltpu.get_barrier_semaphore()
        for where in to.values():
            pl.semaphore_signal(barrier, inc=1, device_id=where, device_id_type=MESH)
        load_grad = pltpu.make_async_copy(grad_hbm, grad_ref, lsem.at[9])
        load_grad.start()
        load_pre = pltpu.make_async_copy(pre_hbm, H.at[q], lsem.at[0])
        load_w2 = pltpu.make_async_copy(w2_hbm, W2, lsem.at[1])
        load_w1 = pltpu.make_async_copy(w1_hbm, W1, lsem.at[2])
        load_pre.start()
        load_w2.start()
        load_w1.start()
        load_grad.wait()

        offset = (seed_ref[0] * jnp.int32(131) + q) * jnp.int32(1640531527)
        row_ids = t * rows + lax.broadcasted_iota(jnp.int32, (rows, block), 0)
        col_ids = lax.broadcasted_iota(jnp.int32, (rows, block), 1)
        base = row_ids * jnp.int32(width) + col_ids + offset
        for j in range(Y):
            hashed = scramble(base + jnp.int32(j * block))
            kept = (jnp.right_shift(hashed, 9) & jnp.int32(1023)) < jnp.int32(922)
            factor = jnp.where(kept, F32(KEEP_SCALE), F32(0.0))
            branch[j] = (grad_ref[:, j * block:(j + 1) * block].astype(F32) * factor).astype(BF)
        G[q, x, z] = branch[q]
        load_pre.wait()
        H[q] = jnp.maximum(H[q], jnp.zeros((), BF))

    with jax.named_scope("barrier"):
        pl.semaphore_wait(barrier, len(to))

    for d, where in ((2, "y2"), (1, "y+"), (3, "y-")):
        send((branch.at[yi(d)], G.at[q, x, z], where), arrival=d - 1)
    count[0] = 3
    waited = set()

    def wait_first(m):
        if m in waited:
            return
        waited.add(m)

        @pl.when(q != m)
        def _():
            pltpu.make_async_remote_copy(
                src_ref=branch.at[0], dst_ref=branch.at[0], send_sem=ssem.at[0],
                recv_sem=rsem.at[(q - m + Y - 1) % Y], device_id=to["y+"], device_id_type=MESH,
            ).wait_recv()

    shared = []
    for src, dst in ((grad_hbm, grad_out), (layer_hbm, layer_out), (gain_hbm, gain_out)):
        shared += send((src, dst, "c"))

    st = {}

    def hidden_step(k):
        def piece(mb, part, rows_from, rows_count):
            return H.at[mb, pl.ds(pl.multiple_of(part * shard + rows_from, half), rows_count)]

        if k == 0:
            st["h1"] = same(H.at[q], "y+", H.at[q], "y-", whole=H.at[pl.ds(0, 2)])
        elif k == 1:
            wait2("h1")
            st["h2"] = same(
                piece(yi(-1), yi(1), 0, half), "y+", piece(yi(1), yi(-1), half, half), "y-",
                whole=H.at[0, pl.ds(0, shard)],
            )
        elif k == 2:
            wait2("h2")
        elif k == 3:
            st["h3"] = same(
                piece(yi(-1), yi(2), 0, shard), "y+", piece(yi(1), yi(2), 0, shard), "y-",
                whole=H.at[0, pl.ds(0, 2 * shard)],
            ) + same(
                piece(yi(-1), yi(3), 0, half), "y+", piece(yi(1), yi(1), half, half), "y-",
                whole=H.at[0, pl.ds(0, shard)],
            )
        else:
            wait2("h3")

    def wait2(key):
        for c in st.pop(key):
            c.wait_recv()

    def same(ref, where, other=None, other_where=None, whole=None):
        if other is None:
            return send((ref, ref, where))
        return send((ref, ref, where), (other, other, other_where), whole=whole)


    groups = ((0,), (1, -1), (2,))
    slot_of = {0: 0, 1: 1, -1: 2, 2: 3}

    def many(parts, two, four):
        return send(*parts, whole=(None, two, None, four)[len(parts) - 1])

    def gather_a(m, k):
        two, four = RAX1.at[m], RA4.at[m]

        def on(g, d):
            parts = []
            for dx in groups[g]:
                up, down = G.at[m, xi(dx), zi(-d), :, A], G.at[m, xi(dx), zi(d), :, A]
                if d < 3 or dx in (0, 1):
                    parts.append((up, up, "z+"))
                if d < 3 or dx in (-1, 2):
                    parts.append((down, down, "z-"))
            st["ga", m, g] = many(parts, two, four)

        if k == 0:
            own = G.at[m, x, z, :, A]
            st["gx1", m] = same(own, "x+", own, "x-", whole=two)
            on(0, 0)
            st["gx2", m] = same(own, "x2")
        elif k == 6:
            for g in range(3):
                wait2(("ga", m, g))
        elif k in (110, 120):
            wait2(("gx1" if k == 110 else "gx2", m))
            on((k - 100) // 10, 0)
        else:
            g = (k - 100) // 10
            wait2(("ga", m, g))
            on(g, k % 10)

    def gather_b(m, k):
        two, four = RBZ.at[m, :, 0], RB2.at[m, 0]

        def piece(dx, dz):
            return G.at[m, xi(dx), zi(dz), :, B]

        def along_z(d):
            parts = [(piece(0, -d), piece(0, -d), "z+")]
            if d < 3:
                parts.append((piece(0, d), piece(0, d), "z-"))
            st["gz", m, d] = many(parts, two, four)

        def along_x(d):
            parts = []
            for dz in ((d,) if d in (0, 4) else (d, -d)):
                parts += [(piece(0, dz), piece(0, dz), w) for w in ("x+", "x-")]
            st["gx", m, d] = many(parts, two, four)

        if k == 0:
            along_z(0)
            along_x(0)
        elif k == 6:
            for d in range(5):
                wait2(("gf", m, d))
        elif k < 105:
            d = k - 100
            wait2(("gz", m, d - 1))
            if d < 4:
                along_z(d)
            along_x(d)
        else:
            d = k - 110
            wait2(("gx", m, d))
            parts = []
            if d < 4:
                parts.append((piece(-1, d), piece(-1, d), "x+"))
            if d > 0:
                parts.append((piece(1, -d), piece(1, -d), "x-"))
            st["gf", m, d] = many(parts, two, four)

    def scatter_a(m, k):
        two, four = RAX1.at[m], RA4.at[m]
        every = slice(None)

        def on(g, step):
            parts, d = [], 4 - step
            for dx in groups[g]:
                i = slot_of[dx]
                if step == 0:
                    parts.append(
                        (N.at[m, xi(dx), zi(4), :, A], RA4.at[m, i // 2, i % 2],
                         "z+" if dx in (0, 1) else "z-")
                    )
                else:
                    parts += [
                        (N.at[m, xi(dx), zi(d), :, A], RA.at[m, 0, d - 1, i], "z+"),
                        (N.at[m, xi(dx), zi(-d), :, A], RA.at[m, 1, d - 1, i], "z-"),
                    ]
            st["sa", m, g] = many(parts, two, four)

        if k == 0:
            norm_part(m, pl.ds(0, early))
            for g in (2, 1, 0):
                on(g, 0)
        elif k == 6:
            wait2(("sx", m, 1))
            wait2(("sx", m, 2))
            index = (m, x, z, every, A)
            total = N[index].astype(F32) + RAX1[m, 0].astype(F32) + RAX1[m, 1].astype(F32)
            N[index] = (total + RAX2[m].astype(F32)).astype(BF)
        else:
            g, step = (k - 100) // 10, k % 10
            d = 4 - step
            wait2(("sa", m, g))
            for dx in groups[g]:
                i = slot_of[dx]
                if step == 1:
                    there = zi(3) if dx in (0, 1) else zi(-3)
                    add((m, xi(dx), there, every, A), RA4[m, i // 2, i % 2])
                elif step < 4:
                    add((m, xi(dx), zi(d), every, A), RA[m, 0, d, i])
                    add((m, xi(dx), zi(-d), every, A), RA[m, 1, d, i])
                else:
                    index = (m, xi(dx), z, every, A)
                    N[index] = (
                        N[index].astype(F32) + RA[m, 0, 0, i].astype(F32) + RA[m, 1, 0, i].astype(F32)
                    ).astype(BF)
            if step < 4:
                on(g, step)
            elif g == 1:
                st["sx", m, 1] = send(
                    (N.at[m, xi(1), z, :, A], RAX1.at[m, 0], "x+"),
                    (N.at[m, xi(-1), z, :, A], RAX1.at[m, 1], "x-"),
                    whole=two,
                )
            elif g == 2:
                st["sx", m, 2] = send((N.at[m, xi(2), z, :, A], RAX2.at[m], "x2"))

    def scatter_b(m, k):
        two, four = RBZ.at[m, :, 0], RB2.at[m, 0]
        every = slice(None)

        def both(d):
            return ((d, d),) if d in (0, 4) else ((d, d), (-d, Z - d))

        def summed(dz, refs):
            index = (m, x, zi(dz), every, B)
            total = N[index].astype(F32)
            for ref in refs:
                total += ref[...].astype(F32)
            N[index] = total.astype(BF)

        if k == 0:
            for d in (4, 3, 2, 1, 0):
                parts = []
                if d < 4:
                    parts.append((N.at[m, xi(2), zi(d), :, B], RB2.at[m, 0, d], "x+"))
                if d > 0:
                    parts.append((N.at[m, xi(2), zi(-d), :, B], RB2.at[m, 1, d - 1], "x-"))
                st["sf", m, d] = many(parts, two, four)
        elif k >= 110:
            d = k - 110
            wait2(("sf", m, d))
            if d < 4:
                add((m, xi(1), zi(d), every, B), RB2[m, 0, d])
            if d > 0:
                add((m, xi(-1), zi(-d), every, B), RB2[m, 1, d - 1])
            parts = []
            for dz, i in both(d):
                parts += [
                    (N.at[m, xi(1), zi(dz), :, B], RB1.at[m, 0, i], "x+"),
                    (N.at[m, xi(-1), zi(dz), :, B], RB1.at[m, 1, i], "x-"),
                ]
            st["sn", m, d] = many(parts, two, four)
        else:
            d = k - 100 if k > 6 else 0
            wait2(("sn", m, d))
            if d < 4:
                wait2(("sz", m, d + 1))
            for dz, i in both(d):
                refs = [RB1.at[m, 0, i], RB1.at[m, 1, i]]
                if d == 3 and dz == 3:
                    refs.append(RBZ4.at[m])
                elif d == 0:
                    refs += [RBZ.at[m, 0, 0], RBZ.at[m, 1, 0]]
                elif d < 3:
                    refs.append(RBZ.at[m, 0 if dz > 0 else 1, d])
                summed(dz, refs)
            if d == 4:
                st["sz", m, 4] = send((N.at[m, x, zi(4), :, B], RBZ4.at[m], "z+"))
            elif d > 0:
                st["sz", m, d] = send(
                    (N.at[m, x, zi(d), :, B], RBZ.at[m, 0, d - 1], "z+"),
                    (N.at[m, x, zi(-d), :, B], RBZ.at[m, 1, d - 1], "z-"),
                    whole=RBZ.at[m, :, d - 1],
                )

    def ag_a(m, k):
        if m in GATHER_FINE:
            return gather_a(m, k)
        key = ("aga", m)
        if k > 0:
            wait2(key)
        if k == 0:
            own = G.at[m, x, z, :, A]
            st[key] = same(own, "x+", own, "x-", whole=RAX1.at[m])
        elif k == 1:
            if m % 2 == 0:
                st[key] = same(G.at[m, xi(-1), z, :, A], "x+")
            else:
                st[key] = same(G.at[m, xi(1), z, :, A], "x-")
        elif k < 5:
            d = k - 2
            st[key] = same(
                G.at[m, :, zi(-d), :, A], "z+", G.at[m, :, zi(d), :, A], "z-", whole=RA.at[m, :, 0]
            )
        elif k == 5:
            st[key] = same(
                G.at[m, pl.ds(0, 2), zi(-3), :, A], "z+", G.at[m, pl.ds(2, 2), zi(3), :, A], "z-",
                whole=RA4.at[m],
            )

    def ag_b(m, k):
        if m in GATHER_FINE:
            return gather_b(m, k)
        key = ("agb", m)
        if k > 0:
            wait2(key)
        if k < 3:
            st[key] = same(
                G.at[m, x, zi(-k), :, B], "z+", G.at[m, x, zi(k), :, B], "z-", whole=RBZ.at[m, :, 0]
            )
        elif k == 3:
            if m % 2 == 0:
                st[key] = same(G.at[m, x, zi(-3), :, B], "z+")
            else:
                st[key] = same(G.at[m, x, zi(3), :, B], "z-")
        elif k == 4:
            own = G.at[m, x, :, :, B]
            st[key] = same(own, "x+", own, "x-", whole=RB1.at[m])
        elif k == 5:
            st[key] = same(
                G.at[m, xi(-1), pl.ds(0, 4), :, B], "x+", G.at[m, xi(1), pl.ds(4, 4), :, B], "x-",
                whole=RB2.at[m],
            )

    parts = ((0, cut, RY1A, RY2A), (cut, hidden_cols - cut, RY1B, RY2B))

    def y_step(j, m, k):
        key = ("y", j, m)
        start, size, R1, R2 = parts[j]
        cols = pl.ds(start, size)
        lo, hi = pl.ds(0, half), pl.ds(half, half)
        if k > 0:
            wait2(key)
        if k == 0:
            if m == 0 and j == 0:
                load_w2.wait()
            part = jnp.dot(G[m].reshape(tok, block), W2[:, cols], preferred_element_type=F32)
            PH[m, :, :, cols] = part.astype(BF).reshape(Y, shard, size)
            st[key] = send(
                (PH.at[m, yi(2), lo, cols], R1.at[m, 0], "y+"),
                (PH.at[m, yi(2), hi, cols], R1.at[m, 1], "y-"),
                whole=R1.at[m],
            )
        elif k == 1:
            PH[m, yi(1), lo, cols] = PH[m, yi(1), lo, cols] + R1[m, 0]
            PH[m, yi(-1), hi, cols] = PH[m, yi(-1), hi, cols] + R1[m, 1]
            st[key] = send(
                (PH.at[m, yi(1), :, cols], R2.at[m, 0], "y+"),
                (PH.at[m, yi(-1), :, cols], R2.at[m, 1], "y-"),
                whole=R2.at[m],
            )
        elif k == 2:
            total = PH[m, q, :, cols].astype(F32) + R2[m, 0].astype(F32) + R2[m, 1].astype(F32)
            mine = pl.ds(pl.multiple_of(q * shard, shard), shard)
            ACT[m, q, :, cols] = jnp.where(
                H[m, mine, cols].astype(F32) > 0, total, F32(0.0)
            ).astype(BF)
            own = ACT.at[m, q, :, cols]
            st[key] = same(own, "y+", own, "y-", whole=R2.at[m])
        elif k == 3:
            st[key] = same(
                ACT.at[m, yi(-1), lo, cols], "y+", ACT.at[m, yi(1), hi, cols], "y-", whole=R1.at[m]
            )

    def norm_part(m, cols):
        part = jnp.dot(ACT[m].reshape(tok, hidden_cols), W1[:, cols], preferred_element_type=F32)
        N[m, :, :, :, cols] = part.astype(BF).reshape(X, Z, rows, cols.size)

    def mm_step(m, k):
        if m == 0:
            load_w1.wait()
        wait2(("y", 0, m))
        wait2(("y", 1, m))
        norm_part(m, pl.ds(early, block - early))

    def add(index, received):
        N[index] = N[index] + received

    def rs_a(m, k):
        if m in SCATTER_FINE:
            return scatter_a(m, k)
        key = ("rsa", m)
        if k > 0:
            wait2(key)
        lo, hi = pl.ds(0, 2), pl.ds(2, 2)
        if k == 0:
            norm_part(m, pl.ds(0, early))
            st[key] = send(
                (N.at[m, lo, zi(4), :, A], RA4.at[m, 0], "z+"),
                (N.at[m, hi, zi(4), :, A], RA4.at[m, 1], "z-"),
                whole=RA4.at[m],
            )
        elif k < 4:
            d = 4 - k
            if k == 1:
                add((m, lo, zi(3), slice(None), A), RA4[m, 0])
                add((m, hi, zi(-3), slice(None), A), RA4[m, 1])
            else:
                add((m, slice(None), zi(d), slice(None), A), RA[m, 0, d])
                add((m, slice(None), zi(-d), slice(None), A), RA[m, 1, d])
            st[key] = send(
                (N.at[m, :, zi(d), :, A], RA.at[m, 0, d - 1], "z+"),
                (N.at[m, :, zi(-d), :, A], RA.at[m, 1, d - 1], "z-"),
                whole=RA.at[m, :, d - 1],
            )
        elif k == 4:
            index = (m, slice(None), z, slice(None), A)
            N[index] = (
                N[index].astype(F32) + RA[m, 0, 0].astype(F32) + RA[m, 1, 0].astype(F32)
            ).astype(BF)
            st[key] = send((N.at[m, xi(2), z, :, A], RAX2.at[m], "x+" if m % 2 == 0 else "x-"))
        elif k == 5:
            far = xi(1) if m % 2 == 0 else xi(-1)
            add((m, far, z, slice(None), A), RAX2[m])
            st[key] = send(
                (N.at[m, xi(1), z, :, A], RAX1.at[m, 0], "x+"),
                (N.at[m, xi(-1), z, :, A], RAX1.at[m, 1], "x-"),
                whole=RAX1.at[m],
            )
        else:
            index = (m, x, z, slice(None), A)
            N[index] = (
                N[index].astype(F32) + RAX1[m, 0].astype(F32) + RAX1[m, 1].astype(F32)
            ).astype(BF)

    def rs_b(m, k):
        if m in SCATTER_FINE:
            return scatter_b(m, k)
        key = ("rsb", m)
        if k > 0:
            wait2(key)
        lo, hi = pl.ds(0, 4), pl.ds(4, 4)
        every = slice(None)
        if k == 0:
            st[key] = send(
                (N.at[m, xi(2), lo, :, B], RB2.at[m, 0], "x+"),
                (N.at[m, xi(2), hi, :, B], RB2.at[m, 1], "x-"),
                whole=RB2.at[m],
            )
        elif k == 1:
            add((m, xi(1), lo, every, B), RB2[m, 0])
            add((m, xi(-1), hi, every, B), RB2[m, 1])
            st[key] = send(
                (N.at[m, xi(1), :, :, B], RB1.at[m, 0], "x+"),
                (N.at[m, xi(-1), :, :, B], RB1.at[m, 1], "x-"),
                whole=RB1.at[m],
            )
        elif k == 2:
            index = (m, x, every, every, B)
            N[index] = (
                N[index].astype(F32) + RB1[m, 0].astype(F32) + RB1[m, 1].astype(F32)
            ).astype(BF)
            st[key] = send((N.at[m, x, zi(4), :, B], RBZ4.at[m], "z+" if m % 2 == 0 else "z-"))
        elif k < 6:
            d = 6 - k
            if k == 3:
                add((m, x, zi(3) if m % 2 == 0 else zi(-3), every, B), RBZ4[m])
            else:
                add((m, x, zi(d), every, B), RBZ[m, 0, d])
                add((m, x, zi(-d), every, B), RBZ[m, 1, d])
            st[key] = send(
                (N.at[m, x, zi(d), :, B], RBZ.at[m, 0, d - 1], "z+"),
                (N.at[m, x, zi(-d), :, B], RBZ.at[m, 1, d - 1], "z-"),
                whole=RBZ.at[m, :, d - 1],
            )
        else:
            index = (m, x, z, every, B)
            N[index] = (
                N[index].astype(F32) + RBZ[m, 0, 0].astype(F32) + RBZ[m, 1, 0].astype(F32)
            ).astype(BF)

    taken = [0] * (block // tile)

    def weight_grad(m, j):
        cols = pl.ds(j * tile, tile)
        mb = yi(m) if WEIGHT_RELATIVE else m
        part = lax.dot_general(
            G[mb, :, :, :, cols].reshape(tok, tile), H[mb], (((0,), (0,)), ((), ())),
            preferred_element_type=F32,
        )
        taken[j] += 1
        if taken[j] == 1:
            WACC[cols] = part
        elif taken[j] < Y:
            WACC[cols] += part
        else:
            WGR[cols] = (WACC[cols] + part).astype(BF)
            c = pltpu.make_async_copy(WGR.at[cols], wg_hbm.at[cols], lsem.at[3 + j])
            c.start()
            outs.append(c)

    outs = []

    last = COPIES - 1
    finished = []

    def finish(m):
        finished.append(m)
        if finished.count(m) == 2:
            send((N.at[m, x, z], final.at[q], (1 - s, t, m)), arrival=last)

    steps = {
        AG_A: ag_a, AG_B: ag_b, RS_A: rs_a, RS_B: rs_b, MM: mm_step,
        Y_LO: functools.partial(y_step, 0), Y_HI: functools.partial(y_step, 1),
    }
    for kind, m, k in ORDER:
        paced = (kind, k) in PACED
        if paced:

            @pl.when(s == 1)
            def _():
                pl.semaphore_wait(pace_sem, 1)

        if kind == WG:
            weight_grad(m, k)
        elif kind == HF:
            hidden_step(k)
        else:
            if kind in (AG_A, AG_B) and k == 0:
                wait_first(m)
            steps[kind](m, k)
            if kind in (RS_A, RS_B) and k == 6:
                finish(m)
        if paced:

            @pl.when(s == 0)
            def _():
                pl.semaphore_signal(pace_sem, inc=1, device_id=to["c"], device_id_type=MESH)


    with jax.named_scope("last"):
        drain()
        for c in outs:
            c.wait()
        for c in shared:
            c.wait_recv()
        pltpu.make_async_remote_copy(
            src_ref=branch, dst_ref=branch, send_sem=ssem.at[0], recv_sem=rsem.at[last],
            device_id=to["c"], device_id_type=MESH,
        ).wait_recv()


PACED = ((Y_LO, 0), (Y_HI, 0), (Y_HI, 1), (Y_HI, 2))

STRIPS = 8


def norm_back(final, grad, layer, gain, wg_in, out, wg_out, fin, up, lay, gai, res, wg, sems):
    strips = [pl.ds(i * (wg.shape[0] // STRIPS), wg.shape[0] // STRIPS) for i in range(STRIPS)]
    ins = [pltpu.make_async_copy(wg_in.at[r], wg.at[r], sems.at[6 + i]) for i, r in enumerate(strips)]
    outs = [pltpu.make_async_copy(wg.at[r], wg_out.at[r], sems.at[6 + i]) for i, r in enumerate(strips)]
    loads = [
        pltpu.make_async_copy(src, dst, sems.at[1 + i])
        for i, (src, dst) in enumerate(((layer, lay), (final, fin), (gain, gai), (grad, up)))
    ]
    for c in loads:
        c.start()
    for c in ins:
        c.start()
    width = lay.shape[1]
    block = width // Y
    loads[0].wait()
    values = lay[...].astype(F32)
    center = values - jnp.mean(values, axis=-1, keepdims=True)
    scale = lax.rsqrt(jnp.mean(center * center, axis=-1, keepdims=True) + NORM_EPS)
    for c in loads[1:]:
        c.wait()
    for i in range(STRIPS):
        ins[i].wait()
        outs[i].start()
    total = jnp.zeros((lay.shape[0], 1), F32)
    dotted = jnp.zeros((lay.shape[0], 1), F32)
    for j in range(Y):
        cols = slice(j * block, (j + 1) * block)
        scaled = fin[j].astype(F32) * gai[:, cols]
        total += jnp.sum(scaled, axis=-1, keepdims=True)
        dotted += jnp.sum(scaled * (center[:, cols] * scale), axis=-1, keepdims=True)
    total = total / width
    dotted = dotted / width
    for j in range(Y):
        cols = slice(j * block, (j + 1) * block)
        scaled = fin[j].astype(F32) * gai[:, cols]
        bracket = scaled - total - (center[:, cols] * scale) * dotted
        res[:, cols] = (up[:, cols].astype(F32) + scale * bracket).astype(BF)
    store = pltpu.make_async_copy(res, out, sems.at[5])
    store.start()
    store.wait()
    for c in outs:
        c.wait()


SPLIT = 640
SLOTS = 48
COPIES = 3 + 3 + 4 + Y * 32 + 4 + 16 * (len(GATHER_FINE) + len(SCATTER_FINE))


def shards(grad_out, drop_seed, layer_in, ln_gain, pre_act, fc1_weight, fc2_weight):
    rows, width = grad_out.shape[2:]
    tok, hidden = pre_act.shape[2:]
    block = width // Y
    a = SPLIT
    b = block - a
    shard = tok // Y
    cut = hidden // 3
    early = block // 3
    anyspace = pl.BlockSpec(memory_space=pl.ANY)
    final, grad_there, layer_there, gain_there, weight_grad = pl.pallas_call(
        functools.partial(kernel, a, cut, early),
        out_shape=(
            jax.ShapeDtypeStruct((Y, rows, block), BF),
            jax.ShapeDtypeStruct((rows, width), BF),
            jax.ShapeDtypeStruct((rows, width), BF),
            jax.ShapeDtypeStruct((1, width), F32),
            jax.ShapeDtypeStruct((block, hidden), BF),
        ),
        in_specs=[pl.BlockSpec(memory_space=pltpu.SMEM)] + [anyspace] * 6,
        out_specs=(anyspace,) * 5,
        scratch_shapes=[
            pltpu.VMEM((rows, width), BF),
            pltpu.VMEM((Y, rows, block), BF),
            pltpu.VMEM((Y, X, Z, rows, block), BF),
            pltpu.VMEM((Y, tok, hidden), BF),
            pltpu.VMEM((hidden, block), BF),
            pltpu.VMEM((block, hidden), BF),
            pltpu.VMEM((Y, Y, shard, hidden), BF),
            pltpu.VMEM((Y, 2, shard // 2, cut), BF),
            pltpu.VMEM((Y, 2, shard, cut), BF),
            pltpu.VMEM((Y, 2, shard // 2, hidden - cut), BF),
            pltpu.VMEM((Y, 2, shard, hidden - cut), BF),
            pltpu.VMEM((Y, Y, shard, hidden), BF),
            pltpu.VMEM((Y, X, Z, rows, block), BF),
            pltpu.VMEM((Y, 2, X // 2, rows, a), BF),
            pltpu.VMEM((Y, 2, 3, X, rows, a), BF),
            pltpu.VMEM((Y, rows, a), BF),
            pltpu.VMEM((Y, 2, rows, a), BF),
            pltpu.VMEM((Y, 2, Z // 2, rows, b), BF),
            pltpu.VMEM((Y, 2, Z, rows, b), BF),
            pltpu.VMEM((Y, rows, b), BF),
            pltpu.VMEM((Y, 2, 3, rows, b), BF),
            pltpu.VMEM((block, hidden), F32),
            pltpu.VMEM((block, hidden), BF),
            pltpu.SemaphoreType.DMA((SLOTS,)),
            pltpu.SemaphoreType.DMA((COPIES,)),
            pltpu.SemaphoreType.DMA((10,)),
            pltpu.SemaphoreType.REGULAR,
        ],
        compiler_params=pltpu.CompilerParams(
            collective_id=0, has_side_effects=True, vmem_limit_bytes=60 * 1024 * 1024
        ),
    )(
        drop_seed, grad_out[0, 0], layer_in[0, 0], ln_gain,
        pre_act[0, 0], fc1_weight[0], fc2_weight[0],
    )
    arriving, weight_grad = pl.pallas_call(
        norm_back,
        out_shape=(
            jax.ShapeDtypeStruct((rows, width), BF),
            jax.ShapeDtypeStruct((block, hidden), BF),
        ),
        in_specs=[anyspace] * 5,
        out_specs=(anyspace,) * 2,
        scratch_shapes=[
            pltpu.VMEM((Y, rows, block), BF),
            pltpu.VMEM((rows, width), BF),
            pltpu.VMEM((rows, width), BF),
            pltpu.VMEM((1, width), F32),
            pltpu.VMEM((rows, width), BF),
            pltpu.VMEM((block, hidden), BF),
            pltpu.SemaphoreType.DMA((6 + STRIPS,)),
        ],
    )(final, grad_there, layer_there, gain_there, weight_grad)
    return (arriving[None, None], weight_grad[None])


def solution(mesh):
    placed = (
        P("section", "dp", "tensor", None),
        P("section"),
        P("section", "dp", "tensor", None),
        P("section", None),
        P("section", "dp", None, "tensor"),
        P("section", "tensor", "dp"),
        P("section", "dp", "tensor"),
    )
    return jax.shard_map(
        shards,
        mesh=mesh,
        in_specs=placed,
        out_specs=(P("section", "dp", "tensor", None), P("section", "dp", "tensor")),
        check_vma=False,
    )
```
